32 devices in a mesh: fold: 4 (over x, core), blk: 8 (over z, y).
Axes of the slice: x: 2, y: 2, z: 4, core: 2. Of those that a mesh axis runs over, the one named last changes fastest.
Arguments:
- fine_rhs: float32 [1536, 32, 128], P(('fold', 'blk')), may hold values from -6 to 6
- fine_tiles: bfloat16 [1536, 5, 128, 128], P(('fold', 'blk')), as said below
- fine_cols: int32 [1536, 5], P(('fold', 'blk')), may hold values from 0 to 1535, as said below
- fine_smoother: bfloat16 [1536, 128, 128], P(('fold', 'blk'))
- fine_map: int32 [1536], P(('fold', 'blk')), may hold values from 0 to 383, as said below
- fine_slots: int32 [1536, 128], P(('fold', 'blk')), may hold values from 0 to 127
- mid_tiles: bfloat16 [384, 5, 128, 128], P(('fold', 'blk'))
- mid_cols: int32 [384, 5], P(('fold', 'blk')), may hold values from 0 to 383, as said below
- mid_smoother: bfloat16 [384, 128, 128], P(('fold', 'blk'))
- mid_map: int32 [384], P(('fold', 'blk')), may hold values from 0 to 95, as said below
- mid_slots: int32 [384, 128], P(('fold', 'blk')), may hold values from 0 to 127
- coarse_tiles: bfloat16 [96, 5, 128, 128], P('blk')
- coarse_cols: int32 [96, 5], P('blk'), may hold values from 0 to 95, as said below
- coarse_smoother: bfloat16 [96, 128, 128], P('blk')
Outputs:
- fine_field: float32 [1536, 32, 128], P(('fold', 'blk'))
- mid_field: float32 [384, 32, 128], P(('fold', 'blk'))
- coarse_field: float32 [96, 32, 128], P('blk')
The draws below stay inside these ranges and needn't reach their ends.
Inputs may be any that keep to these rules, and one draw needn't show every extreme that they name: `fine_cols`: column 0 of each row names the row's own block; every other entry names a level-0 block of a device with the same fold index whose blk index differs by at most one, cyclically. `mid_cols`: column 0 of each row names the row's own block; every other entry names a level-1 block of a device with the same fold index whose blk index differs by at most one, cyclically. `coarse_cols`: column 0 of each row names the row's own block; every other entry names a level-2 block whose blk index differs from the row's by at most one, cyclically. `fine_map`: A level-0 block's level-1 block lies on a device with the same fold index; of the level-0 blocks of one device at most 12 have their level-1 blocks on any one device, and in every fold row some device receives exactly 12 from every device of that row. `mid_map`: A level-1 block's level-2 block lies at the same blk index. `fine_tiles`: each smoother tile is close to half the inverse of the diagonal of the row block's diagonal tile.
All inputs are finite; a program needn't handle non-finite values.
Results may differ from the reference program's by a relative error of at most 0.012.
Values may be sent and summed in bfloat16 or wider, within the bound.
No kernel may reach another device: no remote copies, remote signals or barrier semaphores. Data moves between devices by JAX's collectives and lax.ppermute only.
A program may use at most 128 MiB of HBM per device.

```python
import math
import jax
import jax.numpy as jnp
from jax import lax

VB = 128
R = 32
KT = 5
PRE = 2
POST = 1
COARSE = 8
B0 = 48
B1 = 12
B2 = 12
CAP = 12
NB0 = 1536
NB1 = 384
NB2 = 96
N_FOLD = 4
N_BLK = 8


def level_diagonal(key, count):
    top_value = 2.0
    return jax.random.uniform(jax.random.fold_in(key, 11), (count, VB), jnp.float32, 1.0, top_value)


def level_tiles(key, count):
    diagonal = level_diagonal(key, count)
    spread_value = 0.03
    others = jax.random.normal(jax.random.fold_in(key, 12), (count, KT, VB, VB), jnp.float32) * spread_value
    identity = jnp.eye(VB, dtype=jnp.float32)
    leading = others[:, 0] + identity[None, :, :] * diagonal[:, :, None]
    return jnp.concatenate([leading[:, None], others[:, 1:]], axis=1)


def level_smoother(key, count):
    diagonal = level_diagonal(key, count)
    noise_part = jax.random.normal(jax.random.fold_in(key, 13), (count, VB, VB), jnp.float32) * 0.005
    identity = jnp.eye(VB, dtype=jnp.float32)
    return noise_part + identity[None, :, :] * (0.5 / diagonal)[:, :, None]


def level_columns(key, count, per_device):
    index = jnp.arange(count, dtype=jnp.int32)
    device = index // per_device
    fold_row = device // N_BLK
    blk_pos = device % N_BLK
    stepping = jax.random.randint(jax.random.fold_in(key, 21), (count, KT - 1), -1, 2)
    local_pick = jax.random.randint(jax.random.fold_in(key, 22), (count, KT - 1), 0, per_device)
    neighbour = (blk_pos[:, None] + stepping + N_BLK) % N_BLK
    others = (fold_row[:, None] * N_BLK + neighbour) * per_device + local_pick
    return jnp.concatenate([index[:, None], others], axis=1).astype(jnp.int32)


def draw_fine_tiles(key, part):
    return level_tiles(jax.random.fold_in(key, 100), NB0).astype(jnp.bfloat16)


def draw_fine_smoother(key, part):
    return level_smoother(jax.random.fold_in(key, 100), NB0).astype(jnp.bfloat16)


def draw_mid_tiles(key, part):
    return level_tiles(jax.random.fold_in(key, 200), NB1).astype(jnp.bfloat16)


def draw_mid_smoother(key, part):
    return level_smoother(jax.random.fold_in(key, 200), NB1).astype(jnp.bfloat16)


def draw_coarse_tiles(key, part):
    return level_tiles(jax.random.fold_in(key, 300), NB2).astype(jnp.bfloat16)


def draw_coarse_smoother(key, part):
    return level_smoother(jax.random.fold_in(key, 300), NB2).astype(jnp.bfloat16)


def draw_fine_cols(key, part):
    return level_columns(jax.random.fold_in(key, 110), NB0, B0)


def draw_mid_cols(key, part):
    return level_columns(jax.random.fold_in(key, 210), NB1, B1)


def draw_coarse_cols(key, part):
    return level_columns(jax.random.fold_in(key, 310), NB2, B2)


def draw_fine_map(key, part):
    base_key = jax.random.fold_in(key, 400)
    total_slots = N_BLK * CAP
    hottest = jax.random.randint(jax.random.fold_in(base_key, 1), (N_FOLD,), 0, N_BLK)

    def one_device(device):
        inner = jax.random.fold_in(base_key, device + 10)
        ordering = jax.random.permutation(jax.random.fold_in(inner, 1), total_slots)
        fold_row = device // N_BLK
        chosen = hottest[fold_row]
        scores = jnp.where(ordering // CAP == chosen, total_slots, 0) + jnp.arange(total_slots, dtype=jnp.int32)
        remaining = ordering[jnp.argsort(scores)]
        picks = jnp.concatenate([chosen * CAP + jnp.arange(CAP, dtype=jnp.int32), remaining])[:B0]
        picks = picks[jax.random.permutation(jax.random.fold_in(inner, 2), B0)]
        local_pick = jax.random.randint(jax.random.fold_in(inner, 3), (B0,), 0, B1)
        return (fold_row * N_BLK + picks // CAP) * B1 + local_pick
    mapped = jax.vmap(one_device)(jnp.arange(N_FOLD * N_BLK, dtype=jnp.int32))
    return mapped.reshape(-1).astype(jnp.int32)


def draw_mid_map(key, part):
    base_key = jax.random.fold_in(key, 500)
    index = jnp.arange(NB1, dtype=jnp.int32)
    blk_pos = index // B1 % N_BLK
    local_pick = jax.random.randint(base_key, (NB1,), 0, B2)
    return (blk_pos * B2 + local_pick).astype(jnp.int32)


def touch_ends(values, stream_key, least, high):
    spot = [jax.random.randint(jax.random.fold_in(stream_key, axis), (), 0, length) for axis, length in enumerate(values.shape)]
    longest = values.shape.index(max(values.shape))
    beside = spot[:longest] + [(spot[longest] + 1) % values.shape[longest]] + spot[longest + 1:]
    return values.at[tuple(spot)].set(least).at[tuple(beside)].set(high)


def block_levels(rng, shape, pieces, low, high):
    gain, own = 1.0, jax.random.fold_in(rng, 6)
    for position, parts in pieces:
        heights = jnp.exp(jax.random.uniform(jax.random.fold_in(own, position), (parts,), jnp.float32, low / len(pieces), high / len(pieces)))
        gain = gain * jnp.repeat(heights, shape[position] // parts).reshape([-1 if axis == position else 1 for axis in range(len(shape))])
    return gain


def gaussian(stream_key, extent, deviation, limit, cuts=(), kind=jnp.bfloat16):
    values = jax.random.normal(stream_key, extent, jnp.float32) * deviation
    if len(cuts) > 0:
        values = block_levels(stream_key, extent, cuts, -0.22, 0.18) * values
    return jnp.clip(values, min=-limit, max=limit).astype(kind)


def setup_inputs(seed: int = 0) -> dict:
    arg_keys = jax.random.split(jax.random.key(seed), 15)
    fine_rhs = gaussian(arg_keys[0], (NB0, R, VB), 1.0, 6.0, ((0, 32),), jnp.float32)
    fine_tiles = draw_fine_tiles(jax.random.fold_in(arg_keys[14], 71), 0)
    fine_cols = draw_fine_cols(jax.random.fold_in(arg_keys[14], 71), 0)
    fine_smoother = draw_fine_smoother(jax.random.fold_in(arg_keys[14], 71), 0)
    fine_map = draw_fine_map(jax.random.fold_in(arg_keys[14], 71), 0)
    fine_slots = touch_ends(jax.random.randint(arg_keys[5], (NB0, VB), 0, VB), jax.random.fold_in(arg_keys[5], 1), 0, VB - 1).astype(jnp.int32)
    mid_tiles = draw_mid_tiles(jax.random.fold_in(arg_keys[14], 71), 0)
    mid_cols = draw_mid_cols(jax.random.fold_in(arg_keys[14], 71), 0)
    mid_smoother = draw_mid_smoother(jax.random.fold_in(arg_keys[14], 71), 0)
    mid_map = draw_mid_map(jax.random.fold_in(arg_keys[14], 71), 0)
    mid_slots = touch_ends(jax.random.randint(arg_keys[10], (NB1, VB), 0, VB), jax.random.fold_in(arg_keys[10], 1), 0, VB - 1).astype(jnp.int32)
    coarse_tiles = draw_coarse_tiles(jax.random.fold_in(arg_keys[14], 71), 0)
    coarse_cols = draw_coarse_cols(jax.random.fold_in(arg_keys[14], 71), 0)
    coarse_smoother = draw_coarse_smoother(jax.random.fold_in(arg_keys[14], 71), 0)
    return {"fine_rhs": fine_rhs, "fine_tiles": fine_tiles, "fine_cols": fine_cols, "fine_smoother": fine_smoother, "fine_map": fine_map, "fine_slots": fine_slots, "mid_tiles": mid_tiles, "mid_cols": mid_cols, "mid_smoother": mid_smoother, "mid_map": mid_map, "mid_slots": mid_slots, "coarse_tiles": coarse_tiles, "coarse_cols": coarse_cols, "coarse_smoother": coarse_smoother}


def apply_level(tiles, columns, field):
    rough = field.astype(jnp.bfloat16)
    count, stored = columns.shape
    group = math.gcd(count, 64)

    def one_group(tile_pair):
        group_tiles, group_cols = tile_pair
        picked = rough[group_cols]
        return jnp.einsum("ikuw,ikrw->iru", group_tiles.astype(jnp.float32), picked.astype(jnp.float32))

    result = lax.map(one_group, (tiles.reshape(count // group, group, stored, VB, VB), columns.reshape(count // group, group, stored)))
    return result.reshape(count, R, VB)


def smooth_level(smoother, resid):
    rough = resid.astype(jnp.bfloat16)
    count = smoother.shape[0]
    group = math.gcd(count, 64)

    def one_group(tile_pair):
        group_tiles, group_resid = tile_pair
        return jnp.einsum("iuw,irw->iru", group_tiles.astype(jnp.float32), group_resid.astype(jnp.float32))

    result = lax.map(one_group, (smoother.reshape(count // group, group, VB, VB), rough.reshape(count // group, group, R, VB)))
    return result.reshape(count, R, VB)


def restrict_level(resid, coarse_map, slots, coarse_count):
    count = resid.shape[0]
    flat_rows = resid.transpose(0, 2, 1).reshape(count * VB, R)
    index = (coarse_map[:, None] * VB + slots).reshape(-1).astype(jnp.int32)
    summed = jax.ops.segment_sum(flat_rows, index, num_segments=coarse_count * VB)
    return summed.reshape(coarse_count, VB, R).transpose(0, 2, 1)


def prolong_level(coarse, coarse_map, slots):
    count = coarse_map.shape[0]
    flat_rows = coarse.transpose(0, 2, 1).reshape(-1, R)
    index = (coarse_map[:, None] * VB + slots).reshape(-1).astype(jnp.int32)
    return flat_rows[index].reshape(count, VB, R).transpose(0, 2, 1)


def smooth_sweeps(tiles, columns, smoother, rhs_field, field, sweeps):
    for sweep_turn in range(sweeps):
        field = field + smooth_level(smoother, rhs_field - apply_level(tiles, columns, field))
    return field


def reference(fine_rhs, fine_tiles, fine_cols, fine_smoother, fine_map, fine_slots, mid_tiles, mid_cols, mid_smoother, mid_map, mid_slots, coarse_tiles, coarse_cols, coarse_smoother):
    fine_pre = smooth_level(fine_smoother, fine_rhs)
    fine_pre = smooth_sweeps(fine_tiles, fine_cols, fine_smoother, fine_rhs, fine_pre, PRE - 1)
    mid_rhs = restrict_level(fine_rhs - apply_level(fine_tiles, fine_cols, fine_pre), fine_map, fine_slots, NB1)
    mid_pre = smooth_level(mid_smoother, mid_rhs)
    mid_pre = smooth_sweeps(mid_tiles, mid_cols, mid_smoother, mid_rhs, mid_pre, PRE - 1)
    coarse_rhs = restrict_level(mid_rhs - apply_level(mid_tiles, mid_cols, mid_pre), mid_map, mid_slots, NB2)
    coarse_field = smooth_level(coarse_smoother, coarse_rhs)
    coarse_field = smooth_sweeps(coarse_tiles, coarse_cols, coarse_smoother, coarse_rhs, coarse_field, COARSE - 1)
    mid_field = mid_pre + prolong_level(coarse_field, mid_map, mid_slots)
    mid_field = smooth_sweeps(mid_tiles, mid_cols, mid_smoother, mid_rhs, mid_field, POST)
    fine_field = fine_pre + prolong_level(mid_field, fine_map, fine_slots)
    fine_field = smooth_sweeps(fine_tiles, fine_cols, fine_smoother, fine_rhs, fine_field, POST)
    return (fine_field, mid_field, coarse_field)
```

```python
import functools

import jax
import jax.numpy as jnp
from jax import lax
from jax.experimental import pallas as pl
from jax.experimental.pallas import tpu as pltpu
from jax.sharding import PartitionSpec as P

COARSE = 8
F32 = jnp.float32
BF16 = jnp.bfloat16
NT = (((1,), (1,)), ((), ()))
VMEM = pl.BlockSpec(memory_space=pltpu.VMEM)
SMEM = pl.BlockSpec(memory_space=pltpu.SMEM)
MIB = 1 << 20


def sds(shape, dtype):
    return jax.ShapeDtypeStruct(shape, dtype)


def params(mib):
    return pltpu.CompilerParams(vmem_limit_bytes=mib * MIB)


def times(x, tile):
    return lax.dot_general(x, tile, NT, preferred_element_type=F32)


def row_product(cols_ref, base, x_ref, tiles_ref, i):
    count = tiles_ref.shape[1]
    picked = [x_ref[cols_ref[base + k]] for k in range(count)]
    x = jnp.concatenate(picked, axis=1).astype(BF16)
    t = jnp.concatenate([tiles_ref[i, k] for k in range(count)], axis=1)
    return times(x, t)


def fill(dest, parts):
    at = 0
    for part in parts:
        dest[at : at + part.shape[0]] = part[...].astype(dest.dtype)
        at += part.shape[0]


def in_groups(count):
    return next(g for g in (8, 6, 4, 3, 2, 1) if count % g == 0)


def ring(axis):
    n = lax.axis_size(axis)
    return [(i, (i + 1) % n) for i in range(n)], [((i + 1) % n, i) for i in range(n)]


def halos(value):
    up, down = ring("blk")
    return lax.ppermute(value, "blk", up), lax.ppermute(value, "blk", down)


def fine_first(smoother, rhs):
    n, r, vb = rhs.shape
    g = in_groups(n)

    def kernel(m_ref, rhs_ref, f_ref, h_ref):
        for i in range(g):
            v = times(rhs_ref[i].astype(BF16), m_ref[i])
            f_ref[i] = v
            h_ref[i] = v.astype(BF16)

    field = pl.BlockSpec((g, r, vb), lambda s: (s, 0, 0))
    return pl.pallas_call(
        kernel,
        grid=(n // g,),
        in_specs=[pl.BlockSpec((g, vb, vb), lambda s: (s, 0, 0)), field],
        out_specs=[field, field],
        out_shape=[sds(rhs.shape, F32), sds(rhs.shape, BF16)],
        compiler_params=params(24),
    )(smoother, rhs)


def fine_sweep(cols, x3, tiles, smoother, rhs, field):
    n, r, vb = rhs.shape
    kt = tiles.shape[1]
    g = in_groups(n)

    def kernel(cols_ref, a_ref, b_ref, c_ref, t_ref, m_ref, rhs_ref, v_ref, f_ref, h_ref, x_ref):
        s = pl.program_id(0)

        @pl.when(s == 0)
        def _():
            fill(x_ref, (a_ref, b_ref, c_ref))

        for i in range(g):
            z = rhs_ref[i] - row_product(cols_ref, (s * g + i) * kt, x_ref, t_ref, i)
            v = v_ref[i] + times(z.astype(BF16), m_ref[i])
            f_ref[i] = v
            h_ref[i] = v.astype(BF16)

    whole = pl.BlockSpec((n, r, vb), lambda s, c: (0, 0, 0))
    block = pl.BlockSpec((g, r, vb), lambda s, c: (s, 0, 0))
    return pl.pallas_call(
        kernel,
        grid_spec=pltpu.PrefetchScalarGridSpec(
            num_scalar_prefetch=1,
            grid=(n // g,),
            in_specs=[whole] * 3
            + [
                pl.BlockSpec((g, kt, vb, vb), lambda s, c: (s, 0, 0, 0)),
                pl.BlockSpec((g, vb, vb), lambda s, c: (s, 0, 0)),
                block,
                block,
            ],
            out_specs=[block, block],
            scratch_shapes=[pltpu.VMEM((3 * n, r, vb), BF16)],
        ),
        out_shape=[sds(rhs.shape, F32), sds(rhs.shape, BF16)],
        compiler_params=params(32),
    )(cols, *x3, tiles, smoother, rhs, field)


def one_hot(slots_row, vb):
    return (lax.broadcasted_iota(jnp.int32, (vb, vb), 0) == slots_row).astype(F32).astype(BF16)


def collected(z, slots_row):
    r, vb = z.shape
    high = z.astype(BF16)
    low = (z - high.astype(F32)).astype(BF16)
    both = times(jnp.concatenate([high, low], axis=0), one_hot(slots_row, vb))
    return both[:r] + both[r:]


def fine_restrict(cols, target, x3, tiles, rhs, slots, mids):
    n, r, vb = rhs.shape
    kt = tiles.shape[1]
    g = in_groups(n)
    steps = n // g

    def kernel(cols_ref, to_ref, a_ref, b_ref, c_ref, t_ref, rhs_ref, s_ref, z_ref, o_ref, x_ref, acc_ref):
        s = pl.program_id(0)

        @pl.when(s == 0)
        def _():
            fill(x_ref, (a_ref, b_ref, c_ref))
            acc_ref[...] = jnp.zeros_like(acc_ref)

        for i in range(g):
            z = rhs_ref[i] - row_product(cols_ref, (s * g + i) * kt, x_ref, t_ref, i)
            z_ref[i] = z
            acc_ref[to_ref[s * g + i]] += collected(z, s_ref[i : i + 1, :])

        @pl.when(s == steps - 1)
        def _():
            o_ref[...] = acc_ref[...].astype(BF16)

    whole = pl.BlockSpec((n, r, vb), lambda s, c, t: (0, 0, 0))
    block = pl.BlockSpec((g, r, vb), lambda s, c, t: (s, 0, 0))
    return pl.pallas_call(
        kernel,
        grid_spec=pltpu.PrefetchScalarGridSpec(
            num_scalar_prefetch=2,
            grid=(steps,),
            in_specs=[whole] * 3
            + [
                pl.BlockSpec((g, kt, vb, vb), lambda s, c, t: (s, 0, 0, 0)),
                block,
                pl.BlockSpec((g, vb), lambda s, c, t: (s, 0)),
            ],
            out_specs=[block, pl.BlockSpec((mids, r, vb), lambda s, c, t: (0, 0, 0))],
            scratch_shapes=[pltpu.VMEM((3 * n, r, vb), BF16), pltpu.VMEM((mids, r, vb), F32)],
        ),
        out_shape=[sds(rhs.shape, F32), sds((mids, r, vb), BF16)],
        compiler_params=params(40),
    )(cols, target, *x3, tiles, rhs, slots)


def fine_last(cols, target3, order, slots3, mid_parts, tiles, smoother, resid, field):
    n, r, vb = resid.shape
    kt = tiles.shape[1]
    g = in_groups(n)
    parts = len(mid_parts)
    per = mid_parts[0].shape[0]

    def kernel(cols_ref, to_ref, order_ref, *refs):
        s_ref, mid_refs, (t_ref, m_ref, z_ref, v_ref, f_ref, x_ref, all_ref) = (
            refs[0],
            refs[1 : 1 + parts],
            refs[1 + parts :],
        )
        s = pl.program_id(0)

        @pl.when(s == 0)
        def _():
            for p in range(parts):
                all_ref[pl.ds(order_ref[p] * per, per)] = mid_refs[p][...].astype(F32)

            def some(j, carry):
                for q in range(g):
                    i = j * g + q
                    index = jnp.broadcast_to(s_ref[pl.ds(i, 1), :], (r, vb))
                    x_ref[i] = jnp.take_along_axis(all_ref[to_ref[i]], index, axis=1).astype(BF16)
                return carry

            lax.fori_loop(0, 3 * n // g, some, 0)

        for i in range(g):
            z = z_ref[i] - row_product(cols_ref, (s * g + i) * kt, x_ref, t_ref, i)
            f_ref[i] = v_ref[i] + x_ref[n + s * g + i].astype(F32) + times(z.astype(BF16), m_ref[i])

    def const(*shape):
        return pl.BlockSpec(shape, lambda s, c, t, o: (0,) * len(shape))

    block = pl.BlockSpec((g, r, vb), lambda s, c, t, o: (s, 0, 0))
    return pl.pallas_call(
        kernel,
        grid_spec=pltpu.PrefetchScalarGridSpec(
            num_scalar_prefetch=3,
            grid=(n // g,),
            in_specs=[const(3 * n, vb)]
            + [const(per, r, vb)] * parts
            + [
                pl.BlockSpec((g, kt, vb, vb), lambda s, c, t, o: (s, 0, 0, 0)),
                pl.BlockSpec((g, vb, vb), lambda s, c, t, o: (s, 0, 0)),
                block,
                block,
            ],
            out_specs=[block],
            scratch_shapes=[pltpu.VMEM((3 * n, r, vb), BF16), pltpu.VMEM((parts * per, r, vb), F32)],
        ),
        out_shape=[sds(resid.shape, F32)],
        compiler_params=params(40),
    )(cols, target3, order, slots3, *mid_parts, tiles, smoother, resid, field)[0]


def add_and_smooth(smoother, terms):
    shape = terms[0].shape

    def kernel(m_ref, *refs):
        term_refs, (rhs_ref, f_ref, h_ref) = refs[:-3], refs[-3:]
        for i in range(shape[0]):
            total = term_refs[0][i].astype(F32)
            for t in term_refs[1:]:
                total = total + t[i].astype(F32)
            rhs_ref[i] = total
            v = times(total.astype(BF16), m_ref[i])
            f_ref[i] = v
            h_ref[i] = v.astype(BF16)

    return pl.pallas_call(
        kernel,
        in_specs=[VMEM] * (1 + len(terms)),
        out_specs=[VMEM] * 3,
        out_shape=[sds(shape, F32), sds(shape, F32), sds(shape, BF16)],
        compiler_params=params(16),
    )(smoother, *terms)


def small_sweep(cols, x3, tiles, smoother, rhs, field):
    n, r, vb = rhs.shape
    kt = tiles.shape[1]
    pick = BF16 if r % 16 == 0 else F32

    def kernel(cols_ref, a_ref, b_ref, c_ref, t_ref, m_ref, rhs_ref, v_ref, f_ref, h_ref, x_ref):
        fill(x_ref, (a_ref, b_ref, c_ref))
        for i in range(n):
            z = rhs_ref[i] - row_product(cols_ref, i * kt, x_ref, t_ref, i)
            v = v_ref[i] + times(z.astype(BF16), m_ref[i])
            f_ref[i] = v
            h_ref[i] = v.astype(BF16)

    return pl.pallas_call(
        kernel,
        in_specs=[SMEM] + [VMEM] * 7,
        out_specs=[VMEM] * 2,
        out_shape=[sds(rhs.shape, F32), sds(rhs.shape, BF16)],
        scratch_shapes=[pltpu.VMEM((3 * n, r, vb), pick)],
        compiler_params=params(24),
    )(cols, *x3, tiles, smoother, rhs, field)


def mid_restrict(cols, target, order, x3, tiles, rhs, slots, lows, folds):
    n, r, vb = rhs.shape
    kt = tiles.shape[1]
    share = r // folds

    def kernel(cols_ref, to_ref, order_ref, a_ref, b_ref, c_ref, t_ref, rhs_ref, s_ref, *refs):
        outs, (x_ref, acc_ref, cut_ref) = refs[:folds], refs[folds:]
        fill(x_ref, (a_ref, b_ref, c_ref))
        acc_ref[...] = jnp.zeros_like(acc_ref)
        for i in range(n):
            z = rhs_ref[i] - row_product(cols_ref, i * kt, x_ref, t_ref, i)
            acc_ref[to_ref[i]] += collected(z, s_ref[i : i + 1, :])
        for f in range(folds):
            cut_ref[f] = acc_ref[:, f * share : (f + 1) * share, :]
        for f in range(folds):
            outs[f][...] = cut_ref[order_ref[f]].astype(BF16)

    return pl.pallas_call(
        kernel,
        in_specs=[SMEM] * 3 + [VMEM] * 6,
        out_specs=[VMEM] * folds,
        out_shape=[sds((lows, share, vb), BF16)] * folds,
        scratch_shapes=[
            pltpu.VMEM((3 * n, r, vb), BF16),
            pltpu.VMEM((lows, r, vb), F32),
            pltpu.VMEM((folds, lows, share, vb), F32),
        ],
        compiler_params=params(24),
    )(cols, target, order, *x3, tiles, rhs, slots)


def mid_lift(target, order, parts, field, slots):
    n, r, vb = field.shape
    folds = len(parts)
    lows, share = parts[0].shape[:2]

    def kernel(to_ref, order_ref, *refs):
        part_refs, (v_ref, s_ref, c_ref, f_ref, h_ref, cut_ref) = refs[:folds], refs[folds:]
        for f in range(folds):
            cut_ref[order_ref[f]] = part_refs[f][...].astype(F32)
        for f in range(folds):
            c_ref[:, f * share : (f + 1) * share, :] = cut_ref[f]
        for i in range(n):
            index = jnp.broadcast_to(s_ref[i : i + 1, :], (r, vb))
            v = v_ref[i] + jnp.take_along_axis(c_ref[to_ref[i]], index, axis=1)
            f_ref[i] = v
            h_ref[i] = v.astype(BF16)

    return pl.pallas_call(
        kernel,
        in_specs=[SMEM] * 2 + [VMEM] * (folds + 2),
        out_specs=[VMEM] * 3,
        out_shape=[sds((lows, r, vb), F32), sds(field.shape, F32), sds(field.shape, BF16)],
        scratch_shapes=[pltpu.VMEM((folds, lows, share, vb), F32)],
        compiler_params=params(16),
    )(target, order, *parts, field, slots)


def local_columns(columns, per_device):
    blks = lax.axis_size("blk")
    owner = columns // per_device % blks
    offset = (owner - lax.axis_index("blk") + 1 + blks) % blks
    return (offset * per_device + columns % per_device).reshape(-1)


def on_device(
    fine_rhs,
    fine_tiles,
    fine_cols,
    fine_smoother,
    fine_map,
    fine_slots,
    mid_tiles,
    mid_cols,
    mid_smoother,
    mid_map,
    mid_slots,
    coarse_tiles,
    coarse_cols,
    coarse_smoother,
):
    n0, r, vb = fine_rhs.shape
    n1 = mid_tiles.shape[0]
    n2 = coarse_tiles.shape[0]
    blks, folds = lax.axis_size("blk"), lax.axis_size("fold")
    blk, fold = lax.axis_index("blk"), lax.axis_index("fold")
    cols0 = local_columns(fine_cols, n0)
    cols1 = local_columns(mid_cols, n1)
    cols2 = local_columns(coarse_cols, n2)
    to_mid = fine_map % (blks * n1)
    to_low = mid_map % n2

    v, h = fine_first(fine_smoother, fine_rhs)
    before, after = halos(h)
    map_rows = -(-n0 // vb)
    table = jnp.concatenate(
        [fine_slots, jnp.pad(to_mid, (0, map_rows * vb - n0)).reshape(map_rows, vb)], axis=0
    )
    table_before, table_after = halos(table)
    v, h = fine_sweep(cols0, (before, h, after), fine_tiles, fine_smoother, fine_rhs, v)
    before, after = halos(h)
    resid, sums = fine_restrict(
        cols0, to_mid, (before, h, after), fine_tiles, fine_rhs, fine_slots, blks * n1
    )
    received = lax.all_to_all(
        sums.reshape(blks, n1, r, vb), "blk", split_axis=0, concat_axis=0, tiled=True
    )

    mid_rhs, w, h = add_and_smooth(mid_smoother, [received[k] for k in range(blks)])
    before, after = halos(h)
    w, h = small_sweep(cols1, (before, h, after), mid_tiles, mid_smoother, mid_rhs, w)
    before, after = halos(h)
    there = (fold + jnp.arange(folds, dtype=jnp.int32)) % folds
    back = (fold - jnp.arange(folds, dtype=jnp.int32)) % folds
    cuts = mid_restrict(
        cols1, to_low, there, (before, h, after), mid_tiles, mid_rhs, mid_slots, n2, folds
    )

    shifts = [[(i, (i + k) % folds) for i in range(folds)] for k in range(folds)]
    terms = [cuts[0]] + [lax.ppermute(cuts[k], "fold", shifts[k]) for k in range(1, folds)]
    low_rhs, c, h = add_and_smooth(coarse_smoother, terms)
    for _ in range(COARSE - 1):
        before, after = halos(h)
        c, h = small_sweep(cols2, (before, h, after), coarse_tiles, coarse_smoother, low_rhs, c)
    parts = [h] + [lax.ppermute(h, "fold", shifts[k]) for k in range(1, folds)]

    coarse_field, w, h = mid_lift(to_low, back, parts, w, mid_slots)
    before, after = halos(h)
    mid_field, h = small_sweep(cols1, (before, h, after), mid_tiles, mid_smoother, mid_rhs, w)

    mids = [h] + [
        lax.ppermute(h, "blk", [(i, (i + k) % blks) for i in range(blks)]) for k in range(1, blks)
    ]
    order = (blk - jnp.arange(blks, dtype=jnp.int32)) % blks
    slots3 = jnp.concatenate([table_before[:n0], fine_slots, table_after[:n0]], axis=0)
    target3 = jnp.concatenate(
        [table_before[n0:].reshape(-1)[:n0], to_mid, table_after[n0:].reshape(-1)[:n0]]
    )
    fine_field = fine_last(
        cols0, target3, order, slots3, mids, fine_tiles, fine_smoother, resid, v
    )
    return fine_field, mid_field, coarse_field


def solution(mesh):
    both = ("fold", "blk")
    return jax.shard_map(
        on_device,
        mesh=mesh,
        in_specs=(
            P(both, None, None),
            P(both, None, None, None),
            P(both, None),
            P(both, None, None),
            P(both),
            P(both, None),
            P(both, None, None, None),
            P(both, None),
            P(both, None, None),
            P(both),
            P(both, None),
            P("blk", None, None, None),
            P("blk", None),
            P("blk", None, None),
        ),
        out_specs=(P(both, None, None), P(both, None, None), P("blk", None, None)),
        check_vma=False,
    )
```

```python
import jax
import jax.numpy as jnp
from jax import lax
from jax.experimental import pallas as pl
from jax.experimental.pallas import tpu as pltpu
from jax.sharding import PartitionSpec as P

COARSE = 8
HALVES, CHUNKS = 2, 2
F32 = jnp.float32
BF16 = jnp.bfloat16
NT = (((1,), (1,)), ((), ()))
VMEM = pl.BlockSpec(memory_space=pltpu.VMEM)
SMEM = pl.BlockSpec(memory_space=pltpu.SMEM)
MIB = 1 << 20


def sds(shape, dtype):
    return jax.ShapeDtypeStruct(shape, dtype)


def params(mib):
    return pltpu.CompilerParams(vmem_limit_bytes=mib * MIB)


def times(x, tile):
    return lax.dot_general(x, tile, NT, preferred_element_type=F32)


def first_before(per, folded):
    blks = lax.axis_size("blk")
    blk = lax.axis_index("blk")
    base = lax.axis_index("fold") * (blks * per) if folded else 0
    return base + (blk - 1) * per, blks * per


def row_product(cols_ref, row, ring, x_ref, tiles_ref):
    first, total = ring
    count = tiles_ref.shape[1]
    picked = []
    for k in range(count):
        place = cols_ref[k, row] - first
        place = jnp.where(place < 0, place + total, place)
        place = jnp.where(place >= total, place - total, place)
        picked.append(x_ref[place])
    x = jnp.concatenate(picked, axis=1).astype(BF16)
    t = jnp.concatenate([tiles_ref[row, k] for k in range(count)], axis=1)
    return times(x, t)


def fill(dest, parts, at=0):
    for part in parts:
        dest[pl.ds(at, part.shape[0])] = part[...].astype(dest.dtype)
        at = at + part.shape[0]


def fill_pair(dest, parts, n):
    side = lax.axis_index("blk") % 2
    third = len(parts) // 3
    fill(dest, parts[:third], n)
    fill(dest, parts[third : 2 * third], (1 - side) * (2 * n))
    fill(dest, parts[2 * third :], side * (2 * n))


def in_groups(count):
    return next(g for g in (8, 6, 4, 3, 2, 1) if count % g == 0)


def cost(us):
    return pl.CostEstimate(flops=0, bytes_accessed=int(us * 3.0e6), transcendentals=0)


def halos(value):
    n = lax.axis_size("blk")
    up = [(i, (i + 1) % n) for i in range(n)]
    down = [((i + 1) % n, i) for i in range(n)]
    return lax.ppermute(value, "blk", up), lax.ppermute(value, "blk", down)


def partner(value):
    n = lax.axis_size("blk")
    return lax.ppermute(value, "blk", [(i, i ^ 1) for i in range(n)])


def forwarded(value):
    n = lax.axis_size("blk")
    return lax.ppermute(value, "blk", [(i, (i + 2 - 4 * (i % 2)) % n) for i in range(n)])


def pair_halos(chunks):
    near = [partner(c) for c in chunks]
    return near + [forwarded(c) for c in near]


def store_chunks(i, value, h_refs):
    size = h_refs[0].shape[0]
    for c, h_ref in enumerate(h_refs):

        @pl.when((i >= c * size) & (i < (c + 1) * size))
        def _(c=c, h_ref=h_ref):
            h_ref[pl.ds(i - c * size, value.shape[0])] = value


def fine_first(low, count, chunks, smoother, rhs):
    n, r, vb = rhs.shape
    size = count // chunks
    g = in_groups(size)
    steps = count // g

    def kernel(m_ref, rhs_ref, f_ref, *h_refs):
        def step(j, carry):
            at = j * g
            vs = [
                times(rhs_ref[low + at + i].astype(BF16), m_ref[low + at + i]) for i in range(g)
            ]
            for i in range(g):
                f_ref[at + i] = vs[i]
            store_chunks(at, jnp.stack([v.astype(BF16) for v in vs]), h_refs)
            return carry

        lax.fori_loop(0, steps, step, 0)

    f, *h = pl.pallas_call(
        kernel,
        in_specs=[VMEM] * 2,
        out_specs=[VMEM] * (1 + chunks),
        out_shape=[sds((count, r, vb), F32)] + [sds((size, r, vb), BF16)] * chunks,
        compiler_params=params(12),
        cost_estimate=cost(count * 0.04),
    )(smoother, rhs)
    return f, h


def brought(source, after):
    n = source.shape[0]
    parts = in_groups(n)
    size = n // parts

    def kernel(source_ref, after_ref, copied_ref, sems):
        copies = []
        for p in range(parts):
            at = pl.ds(p * size, size)
            copies.append(pltpu.make_async_copy(source_ref.at[at], copied_ref.at[at], sems.at[p]))
        for copy in copies:
            copy.start()
        for copy in copies:
            copy.wait()

    return pl.pallas_call(
        kernel,
        in_specs=[pl.BlockSpec(memory_space=pl.ANY)] * 2,
        out_specs=VMEM,
        out_shape=sds(source.shape, source.dtype),
        scratch_shapes=[pltpu.SemaphoreType.DMA((parts,))],
        compiler_params=params(12),
        cost_estimate=cost(3),
    )(source, after)


def fine_sweep(low, count, chunks, cols, x_parts, tiles, smoother, rhs, field):
    n, r, vb = rhs.shape
    size = count // chunks
    g = in_groups(size)
    steps = count // g
    parts = len(x_parts)

    def kernel(cols_ref, *refs):
        x_refs, (t_ref, m_ref, rhs_ref, v_ref, f_ref), (*h_refs, x_ref) = (
            refs[:parts],
            refs[parts : parts + 5],
            refs[parts + 5 :],
        )
        fill_pair(x_ref, x_refs, n)
        ring = first_before(n, True)

        def step(j, carry):
            at = j * g
            zs = []
            for i in range(g):
                row = low + at + i
                z = rhs_ref[row] - row_product(cols_ref, row, ring, x_ref, t_ref)
                zs.append(z.astype(BF16))
            vs = [v_ref[at + i] + times(zs[i], m_ref[low + at + i]) for i in range(g)]
            for i in range(g):
                f_ref[at + i] = vs[i]
            store_chunks(at, jnp.stack([v.astype(BF16) for v in vs]), h_refs)
            return carry

        lax.fori_loop(0, steps, step, 0)

    f, *h = pl.pallas_call(
        kernel,
        in_specs=[SMEM] + [VMEM] * (parts + 4),
        out_specs=[VMEM] * (1 + chunks),
        out_shape=[sds((count, r, vb), F32)] + [sds((size, r, vb), BF16)] * chunks,
        scratch_shapes=[pltpu.VMEM((3 * n, r, vb), BF16)],
        compiler_params=params(12),
        cost_estimate=cost(count * 0.15),
    )(cols, *x_parts, tiles, smoother, rhs, field)
    return f, h


def one_hot(slots_row, vb):
    return (lax.broadcasted_iota(jnp.int32, (vb, vb), 0) == slots_row).astype(F32).astype(BF16)


def collected(z, slots_row):
    r, vb = z.shape
    high = z.astype(BF16)
    low = (z - high.astype(F32)).astype(BF16)
    both = times(jnp.concatenate([high, low], axis=0), one_hot(slots_row, vb))
    return both[:r] + both[r:]


def fine_restrict(cols, to_mid, x_parts, tiles, rhs, slots, map_row, n1):
    n, r, vb = rhs.shape
    g = in_groups(n)
    steps = n // g
    parts = len(x_parts)
    blks = lax.axis_size("blk")
    pairs = blks // 2
    half = pairs * n1
    map_rows = -(-n // vb)

    def kernel(cols_ref, to_ref, *refs):
        x_refs, refs = refs[:parts], refs[parts:]
        t_ref, rhs_ref, s_ref, map_ref, z_ref, own_ref, other_ref, table_ref, x_ref, acc_ref = refs
        fill_pair(x_ref, x_refs, n)
        acc_ref[...] = jnp.zeros_like(acc_ref)
        table_ref[:n] = s_ref[...]
        for q in range(map_rows):
            size = min(vb, n - q * vb)
            table_ref[n + q : n + q + 1, :size] = map_ref[:, q * vb : q * vb + size]
        ring = first_before(n, True)
        side = lax.axis_index("blk") % 2
        base = lax.axis_index("fold") * (blks * n1)

        def step(j, carry):
            at = j * g
            zs = [
                rhs_ref[at + i] - row_product(cols_ref, at + i, ring, x_ref, t_ref)
                for i in range(g)
            ]
            for i in range(g):
                z_ref[at + i] = zs[i]
            pieces = [collected(zs[i], s_ref[pl.ds(at + i, 1), :]) for i in range(g)]
            for i in range(g):
                to = to_ref[at + i] - base
                blk = to // n1
                apart = jnp.where(blk % 2 == side, 0, half)
                acc_ref[apart + (blk // 2) * n1 + (to - blk * n1)] += pieces[i]
            return carry

        lax.fori_loop(0, steps, step, 0)
        own_ref[...] = acc_ref[:half]
        other_ref[...] = acc_ref[half:].astype(BF16)

    return pl.pallas_call(
        kernel,
        in_specs=[SMEM] * 2 + [VMEM] * (parts + 4),
        out_specs=[VMEM] * 4,
        out_shape=[
            sds(rhs.shape, F32),
            sds((half, r, vb), F32),
            sds((half, r, vb), BF16),
            sds((n + map_rows, vb), jnp.int32),
        ],
        scratch_shapes=[pltpu.VMEM((3 * n, r, vb), BF16), pltpu.VMEM((2 * half, r, vb), F32)],
        compiler_params=params(16),
        cost_estimate=cost(n * 0.15),
    )(cols, to_mid, *x_parts, tiles, rhs, slots, map_row)


def pair_sums(own, got, per):
    half, r, vb = own.shape
    count = half // per

    def kernel(own_ref, got_ref, *refs):
        pair = lax.axis_index("blk") // 2
        for k in range(count):
            at = pl.ds((pair + k) % count * per, per)
            refs[k][...] = (own_ref[at] + got_ref[at].astype(F32)).astype(BF16)

    return pl.pallas_call(
        kernel,
        in_specs=[VMEM] * 2,
        out_specs=[VMEM] * count,
        out_shape=[sds((per, r, vb), BF16)] * count,
        compiler_params=params(12),
        cost_estimate=cost(1),
    )(own, got)


def fine_last(cols, to_mid, slots, tables, mid_parts, tiles, smoother, resid, fields):
    n, r, vb = resid.shape
    g = in_groups(n)
    steps = n // g
    parts = len(mid_parts)
    half = parts // 2
    n1 = mid_parts[0].shape[0]

    def kernel(cols_ref, to_ref, near_to_ref, far_to_ref, s_ref, near_ref, far_ref, *refs):
        mid_refs, (t_ref, m_ref, z_ref), refs = refs[:parts], refs[parts : parts + 3], refs[parts + 3 :]
        v_refs, (f_ref, x_ref, all_ref) = refs[: len(fields)], refs[len(fields) :]
        fill(f_ref, v_refs)
        blk = lax.axis_index("blk")
        side = blk % 2
        base = lax.axis_index("fold") * (parts * n1)
        for p in range(parts):
            owner = (blk // 2 + half - p % half) % half * 2 + (side if p < half else 1 - side)
            all_ref[pl.ds(owner * n1, n1)] = mid_refs[p][...].astype(F32)

        def lift(start, slots_of, to_of):
            def some(j, carry):
                lifted = []
                for q in range(g):
                    index = jnp.broadcast_to(slots_of[pl.ds(j * g + q, 1), :], (r, vb))
                    h = all_ref[to_of(j * g + q) - base]
                    lifted.append(jnp.take_along_axis(h, index, axis=1))
                for q in range(g):
                    x_ref[start + j * g + q] = lifted[q].astype(BF16)
                return carry

            lax.fori_loop(0, steps, some, 0)

        def from_table(ref):
            if n <= vb:
                return lambda i: ref[n, i]
            return lambda i: ref[n + i // vb, i % vb]

        lift(n, s_ref, lambda i: to_ref[i])
        lift((1 - side) * (2 * n), near_ref, from_table(near_to_ref))
        lift(side * (2 * n), far_ref, from_table(far_to_ref))
        ring = first_before(n, True)

        def step(j, carry):
            at = j * g
            zs = [
                (z_ref[at + i] - row_product(cols_ref, at + i, ring, x_ref, t_ref)).astype(BF16)
                for i in range(g)
            ]
            vs = [
                f_ref[at + i] + x_ref[n + at + i].astype(F32) + times(zs[i], m_ref[at + i])
                for i in range(g)
            ]
            for i in range(g):
                f_ref[at + i] = vs[i]
            return carry

        lax.fori_loop(0, steps, step, 0)

    return pl.pallas_call(
        kernel,
        in_specs=[SMEM] * 4 + [VMEM] * (6 + parts + len(fields)),
        out_specs=VMEM,
        out_shape=sds(resid.shape, F32),
        scratch_shapes=[pltpu.VMEM((3 * n, r, vb), BF16), pltpu.VMEM((parts * n1, r, vb), F32)],
        compiler_params=params(16),
        cost_estimate=cost(n * 0.2),
    )(
        cols,
        to_mid,
        *tables,
        slots,
        *tables,
        *mid_parts,
        tiles,
        smoother,
        resid,
        *fields,
    )


def add_and_smooth(smoother, terms):
    shape = terms[0].shape

    def kernel(m_ref, *refs):
        term_refs, (rhs_ref, f_ref, h_ref) = refs[:-3], refs[-3:]
        totals = []
        for i in range(shape[0]):
            total = term_refs[0][i].astype(F32)
            for t in term_refs[1:]:
                total = total + t[i].astype(F32)
            totals.append(total)
        vs = [times(total.astype(BF16), m_ref[i]) for i, total in enumerate(totals)]
        for i, v in enumerate(vs):
            rhs_ref[i] = totals[i]
            f_ref[i] = v
            h_ref[i] = v.astype(BF16)

    return pl.pallas_call(
        kernel,
        in_specs=[VMEM] * (1 + len(terms)),
        out_specs=[VMEM] * 3,
        out_shape=[sds(shape, F32), sds(shape, F32), sds(shape, BF16)],
        compiler_params=params(12),
        cost_estimate=cost(1),
    )(smoother, *terms)


def small_sweep(folded, cols, x3, tiles, smoother, rhs, field):
    n, r, vb = rhs.shape
    pick = BF16 if r % 16 == 0 else F32

    def kernel(cols_ref, a_ref, b_ref, c_ref, t_ref, m_ref, rhs_ref, v_ref, f_ref, h_ref, x_ref):
        fill(x_ref, (a_ref, b_ref, c_ref))
        ring = first_before(n, folded)
        zs = [
            (rhs_ref[i] - row_product(cols_ref, i, ring, x_ref, t_ref)).astype(BF16)
            for i in range(n)
        ]
        vs = [v_ref[i] + times(zs[i], m_ref[i]) for i in range(n)]
        for i, v in enumerate(vs):
            f_ref[i] = v
            h_ref[i] = v.astype(BF16)

    return pl.pallas_call(
        kernel,
        in_specs=[SMEM] + [VMEM] * 7,
        out_specs=[VMEM] * 2,
        out_shape=[sds(rhs.shape, F32), sds(rhs.shape, BF16)],
        scratch_shapes=[pltpu.VMEM((3 * n, r, vb), pick)],
        compiler_params=params(12),
    )(cols, *x3, tiles, smoother, rhs, field)


def mid_restrict(cols, to_low, x3, tiles, rhs, slots, lows):
    n, r, vb = rhs.shape
    folds = lax.axis_size("fold")
    share = r // folds

    def kernel(cols_ref, to_ref, a_ref, b_ref, c_ref, t_ref, rhs_ref, s_ref, *refs):
        outs, (x_ref, acc_ref, cut_ref) = refs[:folds], refs[folds:]
        fill(x_ref, (a_ref, b_ref, c_ref))
        acc_ref[...] = jnp.zeros_like(acc_ref)
        ring = first_before(n, True)
        zs = [rhs_ref[i] - row_product(cols_ref, i, ring, x_ref, t_ref) for i in range(n)]
        pieces = [collected(zs[i], s_ref[i : i + 1, :]) for i in range(n)]
        base = lax.axis_index("blk") * lows
        for i in range(n):
            acc_ref[to_ref[i] - base] += pieces[i]
        for f in range(folds):
            cut_ref[f] = acc_ref[:, f * share : (f + 1) * share, :]
        for f in range(folds):
            outs[f][...] = cut_ref[(lax.axis_index("fold") + f) % folds].astype(BF16)

    return pl.pallas_call(
        kernel,
        in_specs=[SMEM] * 2 + [VMEM] * 6,
        out_specs=[VMEM] * folds,
        out_shape=[sds((lows, share, vb), BF16)] * folds,
        scratch_shapes=[
            pltpu.VMEM((3 * n, r, vb), BF16),
            pltpu.VMEM((lows, r, vb), F32),
            pltpu.VMEM((folds, lows, share, vb), F32),
        ],
        compiler_params=params(12),
    )(cols, to_low, *x3, tiles, rhs, slots)


def mid_lift(to_low, parts, field, slots):
    n, r, vb = field.shape
    folds = len(parts)
    lows, share = parts[0].shape[:2]

    def kernel(to_ref, *refs):
        part_refs, (v_ref, s_ref, c_ref, f_ref, h_ref, cut_ref) = refs[:folds], refs[folds:]
        for f in range(folds):
            owner = (lax.axis_index("fold") + folds - f) % folds
            cut_ref[owner] = part_refs[f][...].astype(F32)
        for f in range(folds):
            c_ref[:, f * share : (f + 1) * share, :] = cut_ref[f]
        for i in range(n):
            index = jnp.broadcast_to(s_ref[i : i + 1, :], (r, vb))
            low = to_ref[i] - lax.axis_index("blk") * lows
            v = v_ref[i] + jnp.take_along_axis(c_ref[low], index, axis=1)
            f_ref[i] = v
            h_ref[i] = v.astype(BF16)

    return pl.pallas_call(
        kernel,
        in_specs=[SMEM] + [VMEM] * (folds + 2),
        out_specs=[VMEM] * 3,
        out_shape=[sds((lows, r, vb), F32), sds(field.shape, F32), sds(field.shape, BF16)],
        scratch_shapes=[pltpu.VMEM((folds, lows, share, vb), F32)],
        compiler_params=params(16),
    )(to_low, *parts, field, slots)


def on_device(
    fine_rhs,
    fine_tiles,
    fine_cols,
    fine_smoother,
    fine_map,
    fine_slots,
    mid_tiles,
    mid_cols,
    mid_smoother,
    mid_map,
    mid_slots,
    coarse_tiles,
    coarse_cols,
    coarse_smoother,
):
    n0, r, vb = fine_rhs.shape
    n1 = mid_tiles.shape[0]
    n2 = coarse_tiles.shape[0]
    blks, folds = lax.axis_size("blk"), lax.axis_size("fold")
    pairs = blks // 2
    cols0, cols1, cols2 = fine_cols.T, mid_cols.T, coarse_cols.T

    halves, chunks = HALVES, CHUNKS
    count = n0 // halves
    v, h = [], []
    for k in range(halves):
        part, rough = fine_first(k * count, count, chunks, fine_smoother, fine_rhs)
        v.append(part)
        h += rough
    x = h + pair_halos(h)
    fine_tiles = brought(fine_tiles, x[2 * halves * chunks])
    down, h = [], []
    for k in range(halves):
        part, rough = fine_sweep(
            k * count, count, chunks, cols0, x, fine_tiles, fine_smoother, fine_rhs, v[k]
        )
        down.append(part)
        h += rough
    x = h + pair_halos(h)
    resid, own, other, table = fine_restrict(
        cols0, fine_map, x, fine_tiles, fine_rhs, fine_slots, fine_map[None], n1
    )
    steps = [[(i, (i + 2 * k) % blks) for i in range(blks)] for k in range(pairs)]
    got, near = lax.optimization_barrier((partner(other), partner(table)))
    sums = pair_sums(own, got, n1)
    tables = [near, forwarded(near)]
    terms = [sums[0]] + [lax.ppermute(sums[k], "blk", steps[k]) for k in range(1, pairs)]
    terms, tables = lax.optimization_barrier((terms, tables))

    mid_rhs, w, h = add_and_smooth(mid_smoother, terms)
    before, after = halos(h)
    w, h = small_sweep(True, cols1, (before, h, after), mid_tiles, mid_smoother, mid_rhs, w)
    before, after = halos(h)
    cuts = mid_restrict(cols1, mid_map, (before, h, after), mid_tiles, mid_rhs, mid_slots, n2)

    shifts = [[(i, (i + k) % folds) for i in range(folds)] for k in range(folds)]
    terms = [cuts[0]] + [lax.ppermute(cuts[k], "fold", shifts[k]) for k in range(1, folds)]
    low_rhs, c, h = add_and_smooth(coarse_smoother, terms)
    for _ in range(COARSE - 1):
        before, after = halos(h)
        c, h = small_sweep(
            False, cols2, (before, h, after), coarse_tiles, coarse_smoother, low_rhs, c
        )
    parts = [h] + [lax.ppermute(h, "fold", shifts[k]) for k in range(1, folds)]

    coarse_field, w, h = mid_lift(mid_map, parts, w, mid_slots)
    before, after = halos(h)
    mid_field, h = small_sweep(True, cols1, (before, h, after), mid_tiles, mid_smoother, mid_rhs, w)

    mids = [h] + [lax.ppermute(h, "blk", steps[k]) for k in range(1, pairs)]
    mids = mids + [partner(m) for m in mids]
    fine_field = fine_last(
        cols0,
        fine_map,
        fine_slots,
        tables,
        mids,
        fine_tiles,
        fine_smoother,
        resid,
        down,
    )
    return fine_field, mid_field, coarse_field


def solution(mesh):
    both = ("fold", "blk")
    return jax.shard_map(
        on_device,
        mesh=mesh,
        in_specs=(
            P(both, None, None),
            P(both, None, None, None),
            P(both, None),
            P(both, None, None),
            P(both),
            P(both, None),
            P(both, None, None, None),
            P(both, None),
            P(both, None, None),
            P(both),
            P(both, None),
            P("blk", None, None, None),
            P("blk", None),
            P("blk", None, None),
        ),
        out_specs=(P(both, None, None), P(both, None, None), P("blk", None, None)),
        check_vma=False,
    )
```

```python
import jax
import jax.numpy as jnp
from jax import lax
from jax.experimental import pallas as pl
from jax.experimental.pallas import tpu as pltpu
from jax.sharding import PartitionSpec as P

COARSE = 8
HALVES, CHUNKS = 2, 2
F32 = jnp.float32
BF16 = jnp.bfloat16
NT = (((1,), (1,)), ((), ()))
NN = (((1,), (0,)), ((), ()))
ANY = pl.BlockSpec(memory_space=pl.ANY)
VMEM = pl.BlockSpec(memory_space=pltpu.VMEM)
SMEM = pl.BlockSpec(memory_space=pltpu.SMEM)
MIB = 1 << 20


def sds(shape, dtype):
    return jax.ShapeDtypeStruct(shape, dtype)


def params(mib):
    return pltpu.CompilerParams(vmem_limit_bytes=mib * MIB)


def times(x, tile):
    return lax.dot_general(x, tile, NT, preferred_element_type=F32)


def first_before(per, folded):
    blks = lax.axis_size("blk")
    blk = lax.axis_index("blk")
    base = lax.axis_index("fold") * (blks * per) if folded else 0
    return base + (blk - 1) * per, blks * per


def picked(cols_ref, row, ring, x_ref):
    first, total = ring
    blocks = []
    for k in range(cols_ref.shape[0]):
        place = cols_ref[k, row] - first
        place = jnp.where(place < 0, place + total, place)
        place = jnp.where(place >= total, place - total, place)
        blocks.append(x_ref[place])
    return jnp.concatenate(blocks, axis=1).astype(BF16)


def row_product(cols_ref, row, ring, x_ref, tiles_ref):
    t = jnp.concatenate([tiles_ref[row, k] for k in range(tiles_ref.shape[1])], axis=1)
    return times(picked(cols_ref, row, ring, x_ref), t)


def packed_product(cols_ref, row, ring, x_ref, pack_ref):
    kt, vb = pack_ref.shape[1] - 1, pack_ref.shape[2]
    t = pack_ref[row, :kt].reshape(kt * vb, vb)
    x = picked(cols_ref, row, ring, x_ref)
    return lax.dot_general(x, t, NN, preferred_element_type=F32)


def smoothed(z, pack_ref, row):
    last = pack_ref.shape[1] - 1
    return lax.dot_general(z.astype(BF16), pack_ref[row, last], NN, preferred_element_type=F32)


def fill(dest, parts, at=0):
    for part in parts:
        dest[pl.ds(at, part.shape[0])] = part[...].astype(dest.dtype)
        at = at + part.shape[0]


def fill_pair(dest, parts, n):
    side = lax.axis_index("blk") % 2
    third = len(parts) // 3
    fill(dest, parts[:third], n)
    fill(dest, parts[third : 2 * third], (1 - side) * (2 * n))
    fill(dest, parts[2 * third :], side * (2 * n))


def in_groups(count):
    return next(g for g in (8, 6, 4, 3, 2, 1) if count % g == 0)


def cost(us):
    return pl.CostEstimate(flops=0, bytes_accessed=int(us * 3.0e6), transcendentals=0)


def halos(value):
    n = lax.axis_size("blk")
    up = [(i, (i + 1) % n) for i in range(n)]
    down = [((i + 1) % n, i) for i in range(n)]
    return lax.ppermute(value, "blk", up), lax.ppermute(value, "blk", down)


def partner(value):
    n = lax.axis_size("blk")
    return lax.ppermute(value, "blk", [(i, i ^ 1) for i in range(n)])


def forwarded(value):
    n = lax.axis_size("blk")
    return lax.ppermute(value, "blk", [(i, (i + 2 - 4 * (i % 2)) % n) for i in range(n)])


def pair_halos(chunks):
    near = [partner(c) for c in chunks]
    return near + [forwarded(c) for c in near]


def store_chunks(i, value, h_refs):
    size = h_refs[0].shape[0]
    for c, h_ref in enumerate(h_refs):

        @pl.when((i >= c * size) & (i < (c + 1) * size))
        def _(c=c, h_ref=h_ref):
            h_ref[pl.ds(i - c * size, value.shape[0])] = value


def fine_first(low, count, chunks, smoother, rhs):
    n, r, vb = rhs.shape
    size = count // chunks
    g = in_groups(size)
    steps = count // g

    def kernel(m_ref, rhs_ref, f_ref, *h_refs):
        def step(j, carry):
            at = j * g
            vs = [
                times(rhs_ref[low + at + i].astype(BF16), m_ref[low + at + i]) for i in range(g)
            ]
            for i in range(g):
                f_ref[at + i] = vs[i]
            store_chunks(at, jnp.stack([v.astype(BF16) for v in vs]), h_refs)
            return carry

        lax.fori_loop(0, steps, step, 0)

    f, *h = pl.pallas_call(
        kernel,
        in_specs=[VMEM] * 2,
        out_specs=[VMEM] * (1 + chunks),
        out_shape=[sds((count, r, vb), F32)] + [sds((size, r, vb), BF16)] * chunks,
        compiler_params=params(12),
        cost_estimate=cost(count * 0.04),
    )(smoother, rhs)
    return f, h


def brought(source, after):
    n = source.shape[0]
    parts = in_groups(n)
    size = n // parts

    def kernel(source_ref, after_ref, copied_ref, sems):
        copies = []
        for p in range(parts):
            at = pl.ds(p * size, size)
            copies.append(pltpu.make_async_copy(source_ref.at[at], copied_ref.at[at], sems.at[p]))
        for copy in copies:
            copy.start()
        for copy in copies:
            copy.wait()

    return pl.pallas_call(
        kernel,
        in_specs=[ANY] * 2,
        out_specs=VMEM,
        out_shape=sds(source.shape, source.dtype),
        scratch_shapes=[pltpu.SemaphoreType.DMA((parts,))],
        compiler_params=params(12),
        cost_estimate=cost(3),
    )(source, after)


def fine_sweep(low, count, chunks, cols, x_parts, tiles, smoother, rhs, field):
    n, r, vb = rhs.shape
    size = count // chunks
    g = in_groups(size)
    steps = count // g
    parts = len(x_parts)

    def kernel(cols_ref, *refs):
        x_refs, (t_ref, m_ref, rhs_ref, v_ref, f_ref), (*h_refs, x_ref) = (
            refs[:parts],
            refs[parts : parts + 5],
            refs[parts + 5 :],
        )
        fill_pair(x_ref, x_refs, n)
        ring = first_before(n, True)

        def step(j, carry):
            at = j * g
            zs = []
            for i in range(g):
                row = low + at + i
                z = rhs_ref[row] - row_product(cols_ref, row, ring, x_ref, t_ref)
                zs.append(z.astype(BF16))
            vs = [v_ref[at + i] + times(zs[i], m_ref[low + at + i]) for i in range(g)]
            for i in range(g):
                f_ref[at + i] = vs[i]
            store_chunks(at, jnp.stack([v.astype(BF16) for v in vs]), h_refs)
            return carry

        lax.fori_loop(0, steps, step, 0)

    f, *h = pl.pallas_call(
        kernel,
        in_specs=[SMEM] + [VMEM] * (parts + 4),
        out_specs=[VMEM] * (1 + chunks),
        out_shape=[sds((count, r, vb), F32)] + [sds((size, r, vb), BF16)] * chunks,
        scratch_shapes=[pltpu.VMEM((3 * n, r, vb), BF16)],
        compiler_params=params(12),
        cost_estimate=cost(count * 0.15),
    )(cols, *x_parts, tiles, smoother, rhs, field)
    return f, h


def one_hot(slots_row, vb):
    return (lax.broadcasted_iota(jnp.int32, (vb, vb), 0) == slots_row).astype(F32).astype(BF16)


def collected(z, slots_row):
    r, vb = z.shape
    high = z.astype(BF16)
    low = (z - high.astype(F32)).astype(BF16)
    both = times(jnp.concatenate([high, low], axis=0), one_hot(slots_row, vb))
    return both[:r] + both[r:]


def fine_restrict(cols, to_mid, x_parts, pack, rhs, slots, map_row, n1):
    n, r, vb = rhs.shape
    g = in_groups(n)
    steps = n // g
    parts = len(x_parts)
    blks = lax.axis_size("blk")
    pairs = blks // 2
    half = pairs * n1
    map_rows = -(-n // vb)
    cut = (pairs + 1) // 2

    def kernel(cols_ref, to_ref, *refs):
        x_refs, refs = refs[:parts], refs[parts:]
        pack_ref, rhs_ref, s_ref, map_ref, z_ref, own_ref, *others, table_ref, x_ref, acc_ref = refs
        fill_pair(x_ref, x_refs, n)
        acc_ref[...] = jnp.zeros_like(acc_ref)
        table_ref[:n] = s_ref[...]
        for q in range(map_rows):
            size = min(vb, n - q * vb)
            table_ref[n + q : n + q + 1, :size] = map_ref[:, q * vb : q * vb + size]
        ring = first_before(n, True)
        side = lax.axis_index("blk") % 2
        base = lax.axis_index("fold") * (blks * n1)

        def step(j, carry):
            at = j * g
            zs = [
                rhs_ref[at + i] - packed_product(cols_ref, at + i, ring, x_ref, pack_ref)
                for i in range(g)
            ]
            for i in range(g):
                z_ref[at + i] = zs[i]
            pieces = [collected(zs[i], s_ref[pl.ds(at + i, 1), :]) for i in range(g)]
            for i in range(g):
                to = to_ref[at + i] - base
                blk = to // n1
                apart = jnp.where(blk % 2 == side, 0, half)
                acc_ref[apart + (blk // 2) * n1 + (to - blk * n1)] += pieces[i]
            return carry

        lax.fori_loop(0, steps, step, 0)
        own_ref[...] = acc_ref[:half]
        pair = lax.axis_index("blk") // 2
        for q in range(pairs):
            at = pl.ds(half + (pair + pairs - 1 - q) % pairs * n1, n1)
            place = q % cut * n1
            others[q // cut][place : place + n1] = acc_ref[at].astype(BF16)

    return pl.pallas_call(
        kernel,
        in_specs=[SMEM] * 2 + [VMEM] * (parts + 4),
        out_specs=[VMEM] * 5,
        out_shape=[
            sds(rhs.shape, F32),
            sds((half, r, vb), F32),
            sds((cut * n1, r, vb), BF16),
            sds(((pairs - cut) * n1, r, vb), BF16),
            sds((n + map_rows, vb), jnp.int32),
        ],
        scratch_shapes=[pltpu.VMEM((3 * n, r, vb), BF16), pltpu.VMEM((2 * half, r, vb), F32)],
        compiler_params=params(16),
        cost_estimate=cost(n * 0.15),
    )(cols, to_mid, *x_parts, pack, rhs, slots, map_row)


def pair_sums(own, got, last, n1):
    half, r, vb = own.shape
    count = got.shape[0] // n1

    def kernel(own_ref, got_ref, *refs):
        pair = lax.axis_index("blk") // 2
        for k in range(count):
            at = pl.ds((pair + last - k) % (half // n1) * n1, n1)
            total = own_ref[at] + got_ref[k * n1 : (k + 1) * n1].astype(F32)
            refs[k][...] = total.astype(BF16)

    return pl.pallas_call(
        kernel,
        in_specs=[VMEM] * 2,
        out_specs=[VMEM] * count,
        out_shape=[sds((n1, r, vb), BF16)] * count,
        compiler_params=params(12),
        cost_estimate=cost(0.2),
    )(own, got)


def fine_last(cols, to_mid, slots, tables, mid_parts, pack, resid, fields, others):
    n, r, vb = resid.shape
    g = in_groups(n)
    steps = n // g
    parts = len(mid_parts)
    half = parts // 2
    n1 = mid_parts[0].shape[0]

    def kernel(cols_ref, to_ref, near_to_ref, far_to_ref, s_ref, near_ref, far_ref, *refs):
        mid_refs, (pack_ref, z_ref), refs = refs[:parts], refs[parts : parts + 2], refs[parts + 2 :]
        v_refs, refs = refs[: len(fields)], refs[len(fields) :]
        other_refs, (out_hbm, *other_hbm), (f_ref, x_ref, all_ref, sems, other_sems) = (
            refs[: len(others)],
            refs[len(others) : 2 * len(others) + 1],
            refs[2 * len(others) + 1 :],
        )
        other_copies = [
            pltpu.make_async_copy(source, dest, other_sems.at[q])
            for q, (source, dest) in enumerate(zip(other_refs, other_hbm))
        ]
        for copy in other_copies:
            copy.start()

        def out_copy(j):
            at = pl.ds(j * g, g)
            return pltpu.make_async_copy(f_ref.at[at], out_hbm.at[at], sems.at[j])

        fill(f_ref, v_refs)
        blk = lax.axis_index("blk")
        side = blk % 2
        base = lax.axis_index("fold") * (parts * n1)
        for p in range(parts):
            owner = (blk // 2 + half - p % half) % half * 2 + (side if p < half else 1 - side)
            all_ref[pl.ds(owner * n1, n1)] = mid_refs[parts - 1 - p][...].astype(F32)

        def lift(start, slots_of, to_of):
            def some(j, carry):
                lifted = []
                for q in range(g):
                    index = jnp.broadcast_to(slots_of[pl.ds(j * g + q, 1), :], (r, vb))
                    h = all_ref[to_of(j * g + q) - base]
                    lifted.append(jnp.take_along_axis(h, index, axis=1))
                for q in range(g):
                    x_ref[start + j * g + q] = lifted[q].astype(BF16)
                return carry

            lax.fori_loop(0, steps, some, 0)

        def from_table(ref):
            if n <= vb:
                return lambda i: ref[n, i]
            return lambda i: ref[n + i // vb, i % vb]

        lift(n, s_ref, lambda i: to_ref[i])
        lift((1 - side) * (2 * n), near_ref, from_table(near_to_ref))
        lift(side * (2 * n), far_ref, from_table(far_to_ref))
        ring = first_before(n, True)

        def step(j, carry):
            at = j * g
            zs = [
                z_ref[at + i] - packed_product(cols_ref, at + i, ring, x_ref, pack_ref)
                for i in range(g)
            ]
            vs = [
                f_ref[at + i] + x_ref[n + at + i].astype(F32) + smoothed(zs[i], pack_ref, at + i)
                for i in range(g)
            ]
            for i in range(g):
                f_ref[at + i] = vs[i]
            out_copy(j).start()
            return carry

        lax.fori_loop(0, steps, step, 0)
        for j in range(steps):
            out_copy(j).wait()
        for copy in other_copies:
            copy.wait()

    return pl.pallas_call(
        kernel,
        in_specs=[SMEM] * 4 + [VMEM] * (5 + parts + len(fields) + len(others)),
        out_specs=[ANY] * (1 + len(others)),
        out_shape=[sds(resid.shape, F32)] + [sds(a.shape, a.dtype) for a in others],
        scratch_shapes=[
            pltpu.VMEM((n, r, vb), F32),
            pltpu.VMEM((3 * n, r, vb), BF16),
            pltpu.VMEM((parts * n1, r, vb), F32),
            pltpu.SemaphoreType.DMA((steps,)),
            pltpu.SemaphoreType.DMA((len(others),)),
        ],
        compiler_params=params(16),
        cost_estimate=cost(n * 0.2),
    )(
        cols,
        to_mid,
        *tables,
        slots,
        *tables,
        *mid_parts[::-1],
        pack,
        resid,
        *fields,
        *others,
    )


def packed(tiles, smoother, after):
    n, kt, vb, _ = tiles.shape

    def kernel(t_ref, m_ref, after_ref, o_ref):
        def one(i, carry):
            for k in range(kt):
                o_ref[i, k] = t_ref[i, k].T
            o_ref[i, kt] = m_ref[i].T
            return carry

        lax.fori_loop(0, n, one, 0)

    return pl.pallas_call(
        kernel,
        in_specs=[VMEM] * 2 + [ANY],
        out_specs=VMEM,
        out_shape=sds((n, kt + 1, vb, vb), BF16),
        compiler_params=params(12),
        cost_estimate=cost(2),
    )(tiles, smoother, after)


def add_and_smooth(pack, terms):
    shape = terms[0].shape

    def kernel(pack_ref, *refs):
        term_refs, (rhs_ref, f_ref, h_ref) = refs[:-3], refs[-3:]
        totals = []
        for i in range(shape[0]):
            total = term_refs[0][i].astype(F32)
            for t in term_refs[1:]:
                total = total + t[i].astype(F32)
            totals.append(total)
        vs = [smoothed(total, pack_ref, i) for i, total in enumerate(totals)]
        for i, v in enumerate(vs):
            rhs_ref[i] = totals[i]
            f_ref[i] = v
            h_ref[i] = v.astype(BF16)

    return pl.pallas_call(
        kernel,
        in_specs=[VMEM] * (1 + len(terms)),
        out_specs=[VMEM] * 3,
        out_shape=[sds(shape, F32), sds(shape, F32), sds(shape, BF16)],
        compiler_params=params(12),
        cost_estimate=cost(0.3),
    )(pack, *terms)


def small_sweep(folded, cols, x3, pack, rhs, field, last=False):
    n, r, vb = rhs.shape
    pick = BF16 if r % 16 == 0 else F32
    kinds = [BF16] if last else [BF16, F32]

    def kernel(cols_ref, c_ref, b_ref, a_ref, pack_ref, rhs_ref, v_ref, *refs):
        out_refs, x_ref = refs[:-1], refs[-1]
        fill(x_ref, (a_ref, b_ref, c_ref))
        ring = first_before(n, folded)
        zs = [rhs_ref[i] - packed_product(cols_ref, i, ring, x_ref, pack_ref) for i in range(n)]
        vs = [v_ref[i] + smoothed(zs[i], pack_ref, i) for i in range(n)]
        for i, v in enumerate(vs):
            for out_ref in out_refs:
                out_ref[i] = v.astype(out_ref.dtype)

    return pl.pallas_call(
        kernel,
        in_specs=[SMEM] + [VMEM] * 6,
        out_specs=[VMEM] * len(kinds),
        out_shape=[sds(rhs.shape, kind) for kind in kinds],
        scratch_shapes=[pltpu.VMEM((3 * n, r, vb), pick)],
        compiler_params=params(12),
        cost_estimate=cost(1),
    )(cols, *x3[::-1], pack, rhs, field)


def mid_restrict(cols, to_low, x3, pack, rhs, slots, lows):
    n, r, vb = rhs.shape
    folds = lax.axis_size("fold")
    share = r // folds

    def kernel(cols_ref, to_ref, c_ref, b_ref, a_ref, pack_ref, rhs_ref, s_ref, *refs):
        outs, (x_ref, acc_ref, cut_ref) = refs[:folds], refs[folds:]
        fill(x_ref, (a_ref, b_ref, c_ref))
        acc_ref[...] = jnp.zeros_like(acc_ref)
        ring = first_before(n, True)
        zs = [rhs_ref[i] - packed_product(cols_ref, i, ring, x_ref, pack_ref) for i in range(n)]
        pieces = [collected(zs[i], s_ref[i : i + 1, :]) for i in range(n)]
        base = lax.axis_index("blk") * lows
        for i in range(n):
            acc_ref[to_ref[i] - base] += pieces[i]
        for f in range(folds):
            cut_ref[f] = acc_ref[:, f * share : (f + 1) * share, :]
        for f in range(folds):
            outs[f][...] = cut_ref[(lax.axis_index("fold") + f) % folds].astype(BF16)

    return pl.pallas_call(
        kernel,
        in_specs=[SMEM] * 2 + [VMEM] * 6,
        out_specs=[VMEM] * folds,
        out_shape=[sds((lows, share, vb), BF16)] * folds,
        scratch_shapes=[
            pltpu.VMEM((3 * n, r, vb), BF16),
            pltpu.VMEM((lows, r, vb), F32),
            pltpu.VMEM((folds, lows, share, vb), F32),
        ],
        compiler_params=params(12),
    )(cols, to_low, *x3[::-1], pack, rhs, slots)


def mid_lift(to_low, parts, field, slots):
    n, r, vb = field.shape
    folds = len(parts)
    lows, share = parts[0].shape[:2]

    def kernel(to_ref, *refs):
        part_refs, (v_ref, s_ref, c_ref, f_ref, h_ref, cut_ref) = refs[:folds], refs[folds:]
        for f in range(folds):
            owner = (lax.axis_index("fold") + folds - f) % folds
            cut_ref[owner] = part_refs[f][...].astype(F32)
        for f in range(folds):
            c_ref[:, f * share : (f + 1) * share, :] = cut_ref[f]
        for i in range(n):
            index = jnp.broadcast_to(s_ref[i : i + 1, :], (r, vb))
            low = to_ref[i] - lax.axis_index("blk") * lows
            v = v_ref[i] + jnp.take_along_axis(c_ref[low], index, axis=1)
            f_ref[i] = v
            h_ref[i] = v.astype(BF16)

    return pl.pallas_call(
        kernel,
        in_specs=[SMEM] + [VMEM] * (folds + 2),
        out_specs=[VMEM] * 3,
        out_shape=[sds((lows, r, vb), F32), sds(field.shape, F32), sds(field.shape, BF16)],
        scratch_shapes=[pltpu.VMEM((folds, lows, share, vb), F32)],
        compiler_params=params(16),
    )(to_low, *parts, field, slots)


def on_device(
    fine_rhs,
    fine_tiles,
    fine_cols,
    fine_smoother,
    fine_map,
    fine_slots,
    mid_tiles,
    mid_cols,
    mid_smoother,
    mid_map,
    mid_slots,
    coarse_tiles,
    coarse_cols,
    coarse_smoother,
):
    n0, r, vb = fine_rhs.shape
    n1 = mid_tiles.shape[0]
    n2 = coarse_tiles.shape[0]
    blks, folds = lax.axis_size("blk"), lax.axis_size("fold")
    pairs = blks // 2
    cols0, cols1, cols2 = fine_cols.T, mid_cols.T, coarse_cols.T

    halves, chunks = HALVES, CHUNKS
    count = n0 // halves
    v, h = [], []
    for k in range(halves):
        part, rough = fine_first(k * count, count, chunks, fine_smoother, fine_rhs)
        v.append(part)
        h += rough
    x = h + pair_halos(h)
    fine_tiles = brought(fine_tiles, x[2 * halves * chunks])
    down, h = [], []
    for k in range(halves):
        part, rough = fine_sweep(
            k * count, count, chunks, cols0, x, fine_tiles, fine_smoother, fine_rhs, v[k]
        )
        down.append(part)
        h += rough
    x = h + pair_halos(h)
    fine_pack = packed(fine_tiles, fine_smoother, x[2 * halves * chunks - 1])
    resid, own, *others, table = fine_restrict(
        cols0, fine_map, x, fine_pack, fine_rhs, fine_slots, fine_map[None], n1
    )
    steps = [[(i, (i + 2 * k) % blks) for i in range(blks)] for k in range(pairs)]
    late = partner(others[1])
    early = partner(others[0])
    early, near = lax.optimization_barrier((early, partner(table)))
    mid_pack = packed(mid_tiles, mid_smoother, others[0])
    low_pack = packed(coarse_tiles, coarse_smoother, others[0])
    early, mid_pack, low_pack = lax.optimization_barrier((early, mid_pack, low_pack))
    cut = others[1].shape[0] // n1
    sums = pair_sums(own, early, pairs - 1, n1) + pair_sums(own, late, cut - 1, n1)
    sums = sums[::-1]
    tables = [near, forwarded(near)]
    terms = [sums[0]] + [lax.ppermute(sums[k], "blk", steps[k]) for k in range(1, pairs)]
    terms, tables = lax.optimization_barrier((terms, tables))

    mid_rhs, w, h = add_and_smooth(mid_pack, terms)
    before, after = halos(h)
    w, h = small_sweep(True, cols1, (before, h, after), mid_pack, mid_rhs, w)[::-1]
    before, after = halos(h)
    cuts = mid_restrict(cols1, mid_map, (before, h, after), mid_pack, mid_rhs, mid_slots, n2)

    shifts = [[(i, (i + k) % folds) for i in range(folds)] for k in range(folds)]
    terms = [cuts[0]] + [lax.ppermute(cuts[k], "fold", shifts[k]) for k in range(1, folds)]
    low_rhs, c, h = add_and_smooth(low_pack, terms)
    for k in range(1, COARSE):
        before, after = halos(h)
        h, *c = small_sweep(
            False, cols2, (before, h, after), low_pack, low_rhs, c, last=k == COARSE - 1
        )
        c = c[0] if c else None
    parts = [h] + [lax.ppermute(h, "fold", shifts[k]) for k in range(1, folds)]

    coarse_field, w, h = mid_lift(mid_map, parts, w, mid_slots)
    before, after = halos(h)
    h, mid_field = small_sweep(True, cols1, (before, h, after), mid_pack, mid_rhs, w)

    far_mids = [lax.ppermute(h, "blk", steps[k]) for k in range(pairs - 1, 0, -1)]
    mids = [h] + far_mids[::-1]
    mids = mids + [partner(m) for m in far_mids + [h]][::-1]
    fine_field, mid_field, coarse_field = fine_last(
        cols0,
        fine_map,
        fine_slots,
        tables,
        mids,
        fine_pack,
        resid,
        down,
        (mid_field, coarse_field),
    )
    return fine_field, mid_field, coarse_field


def solution(mesh):
    both = ("fold", "blk")
    return jax.shard_map(
        on_device,
        mesh=mesh,
        in_specs=(
            P(both, None, None),
            P(both, None, None, None),
            P(both, None),
            P(both, None, None),
            P(both),
            P(both, None),
            P(both, None, None, None),
            P(both, None),
            P(both, None, None),
            P(both),
            P(both, None),
            P("blk", None, None, None),
            P("blk", None),
            P("blk", None, None),
        ),
        out_specs=(P(both, None, None), P(both, None, None), P("blk", None, None)),
        check_vma=False,
    )
```

```python
import jax
import jax.numpy as jnp
from jax import lax
from jax.experimental import pallas as pl
from jax.experimental.pallas import tpu as pltpu
from jax.sharding import PartitionSpec as P

COARSE = 8
HALVES, CHUNKS = 2, 2
F32 = jnp.float32
BF16 = jnp.bfloat16
NT = (((1,), (1,)), ((), ()))
NN = (((1,), (0,)), ((), ()))
ANY = pl.BlockSpec(memory_space=pl.ANY)
VMEM = pl.BlockSpec(memory_space=pltpu.VMEM)
SMEM = pl.BlockSpec(memory_space=pltpu.SMEM)
MIB = 1 << 20


def sds(shape, dtype):
    return jax.ShapeDtypeStruct(shape, dtype)


def params(mib):
    return pltpu.CompilerParams(vmem_limit_bytes=mib * MIB)


def times(x, tile):
    return lax.dot_general(x, tile, NT, preferred_element_type=F32)


def first_before(per, folded):
    blks = lax.axis_size("blk")
    blk = lax.axis_index("blk")
    base = lax.axis_index("fold") * (blks * per) if folded else 0
    return base + (blk - 1) * per, blks * per


def picked(cols_ref, row, ring, x_ref):
    first, total = ring
    blocks = []
    for k in range(cols_ref.shape[0]):
        place = cols_ref[k, row] - first
        place = jnp.where(place < 0, place + total, place)
        place = jnp.where(place >= total, place - total, place)
        blocks.append(x_ref[place])
    return jnp.concatenate(blocks, axis=1).astype(BF16)


def row_product(cols_ref, row, ring, x_ref, tiles_ref):
    t = jnp.concatenate([tiles_ref[row, k] for k in range(tiles_ref.shape[1])], axis=1)
    return times(picked(cols_ref, row, ring, x_ref), t)


def packed_product(cols_ref, row, ring, x_ref, pack_ref):
    kt, vb = pack_ref.shape[1] - 1, pack_ref.shape[2]
    t = pack_ref[row, :kt].reshape(kt * vb, vb)
    x = picked(cols_ref, row, ring, x_ref)
    return lax.dot_general(x, t, NN, preferred_element_type=F32)


def smoothed(z, pack_ref, row):
    last = pack_ref.shape[1] - 1
    return lax.dot_general(z.astype(BF16), pack_ref[row, last], NN, preferred_element_type=F32)


def fill(dest, parts, at=0):
    for part in parts:
        dest[pl.ds(at, part.shape[0])] = part[...].astype(dest.dtype)
        at = at + part.shape[0]


def fill_pair(dest, parts, n):
    side = lax.axis_index("blk") % 2
    third = len(parts) // 3
    fill(dest, parts[:third], n)
    fill(dest, parts[third : 2 * third], (1 - side) * (2 * n))
    fill(dest, parts[2 * third :], side * (2 * n))


def in_groups(count):
    return next(g for g in (12, 8, 6, 4, 3, 2, 1) if count % g == 0)


def cost(us):
    return pl.CostEstimate(flops=0, bytes_accessed=int(us * 3.0e6), transcendentals=0)


def halos(value):
    n = lax.axis_size("blk")
    up = [(i, (i + 1) % n) for i in range(n)]
    down = [((i + 1) % n, i) for i in range(n)]
    return lax.ppermute(value, "blk", up), lax.ppermute(value, "blk", down)


def partner(value):
    n = lax.axis_size("blk")
    return lax.ppermute(value, "blk", [(i, i ^ 1) for i in range(n)])


def forwarded(value):
    n = lax.axis_size("blk")
    return lax.ppermute(value, "blk", [(i, (i + 2 - 4 * (i % 2)) % n) for i in range(n)])


def pair_halos(chunks):
    near = [partner(c) for c in chunks]
    return near + [forwarded(c) for c in near]


def store_chunks(i, value, h_refs):
    size = h_refs[0].shape[0]
    for c, h_ref in enumerate(h_refs):

        @pl.when((i >= c * size) & (i < (c + 1) * size))
        def _(c=c, h_ref=h_ref):
            h_ref[pl.ds(i - c * size, value.shape[0])] = value


def fine_first(low, count, chunks, smoother, rhs):
    n, r, vb = rhs.shape
    size = count // chunks
    g = in_groups(size)
    steps = count // g

    def kernel(m_ref, rhs_ref, f_ref, *h_refs):
        def step(j, carry):
            at = j * g
            vs = [
                times(rhs_ref[low + at + i].astype(BF16), m_ref[low + at + i]) for i in range(g)
            ]
            for i in range(g):
                f_ref[at + i] = vs[i]
            store_chunks(at, jnp.stack([v.astype(BF16) for v in vs]), h_refs)
            return carry

        lax.fori_loop(0, steps, step, 0)

    f, *h = pl.pallas_call(
        kernel,
        in_specs=[VMEM] * 2,
        out_specs=[VMEM] * (1 + chunks),
        out_shape=[sds((count, r, vb), F32)] + [sds((size, r, vb), BF16)] * chunks,
        compiler_params=params(12),
        cost_estimate=cost(count * 0.04),
    )(smoother, rhs)
    return f, h


def brought(source, after):
    n = source.shape[0]
    parts = in_groups(n)
    size = n // parts

    def kernel(source_ref, after_ref, copied_ref, sems):
        copies = []
        for p in range(parts):
            at = pl.ds(p * size, size)
            copies.append(pltpu.make_async_copy(source_ref.at[at], copied_ref.at[at], sems.at[p]))
        for copy in copies:
            copy.start()
        for copy in copies:
            copy.wait()

    return pl.pallas_call(
        kernel,
        in_specs=[ANY] * 2,
        out_specs=VMEM,
        out_shape=sds(source.shape, source.dtype),
        scratch_shapes=[pltpu.SemaphoreType.DMA((parts,))],
        compiler_params=params(12),
        cost_estimate=cost(3),
    )(source, after)


def fine_sweep(low, count, chunks, cols, x_parts, tiles, smoother, rhs, field):
    n, r, vb = rhs.shape
    size = count // chunks
    g = in_groups(size)
    steps = count // g
    parts = len(x_parts)

    def kernel(cols_ref, *refs):
        x_refs, (t_ref, m_ref, rhs_ref, v_ref, f_ref), (*h_refs, x_ref) = (
            refs[:parts],
            refs[parts : parts + 5],
            refs[parts + 5 :],
        )
        fill_pair(x_ref, x_refs, n)
        ring = first_before(n, True)

        def step(j, carry):
            at = j * g
            zs = []
            for i in range(g):
                row = low + at + i
                z = rhs_ref[row] - row_product(cols_ref, row, ring, x_ref, t_ref)
                zs.append(z.astype(BF16))
            vs = [v_ref[at + i] + times(zs[i], m_ref[low + at + i]) for i in range(g)]
            for i in range(g):
                f_ref[at + i] = vs[i]
            store_chunks(at, jnp.stack([v.astype(BF16) for v in vs]), h_refs)
            return carry

        lax.fori_loop(0, steps, step, 0)

    f, *h = pl.pallas_call(
        kernel,
        in_specs=[SMEM] + [VMEM] * (parts + 4),
        out_specs=[VMEM] * (1 + chunks),
        out_shape=[sds((count, r, vb), F32)] + [sds((size, r, vb), BF16)] * chunks,
        scratch_shapes=[pltpu.VMEM((3 * n, r, vb), BF16)],
        compiler_params=params(12),
        cost_estimate=cost(count * 0.15),
    )(cols, *x_parts, tiles, smoother, rhs, field)
    return f, h


def one_hot(slots_row, vb):
    return (lax.broadcasted_iota(jnp.int32, (vb, vb), 0) == slots_row).astype(F32).astype(BF16)


def collected(z, slots_row):
    r, vb = z.shape
    high = z.astype(BF16)
    low = (z - high.astype(F32)).astype(BF16)
    both = times(jnp.concatenate([high, low], axis=0), one_hot(slots_row, vb))
    return both[:r] + both[r:]


def fine_restrict(cols, to_mid, x_parts, pack, rhs, slots, map_row, n1):
    n, r, vb = rhs.shape
    g = in_groups(n)
    steps = n // g
    parts = len(x_parts)
    blks = lax.axis_size("blk")
    pairs = blks // 2
    half = pairs * n1
    map_rows = -(-n // vb)
    cut = (pairs + 1) // 2

    def kernel(cols_ref, to_ref, *refs):
        x_refs, refs = refs[:parts], refs[parts:]
        pack_ref, rhs_ref, s_ref, map_ref, z_ref, own_ref, *others, table_ref, x_ref, acc_ref = refs
        fill_pair(x_ref, x_refs, n)
        acc_ref[...] = jnp.zeros_like(acc_ref)
        table_ref[:n] = s_ref[...]
        for q in range(map_rows):
            size = min(vb, n - q * vb)
            table_ref[n + q : n + q + 1, :size] = map_ref[:, q * vb : q * vb + size]
        ring = first_before(n, True)
        side = lax.axis_index("blk") % 2
        base = lax.axis_index("fold") * (blks * n1)

        def step(j, carry):
            at = j * g
            zs = [
                rhs_ref[at + i] - packed_product(cols_ref, at + i, ring, x_ref, pack_ref)
                for i in range(g)
            ]
            for i in range(g):
                z_ref[at + i] = zs[i]
            pieces = [collected(zs[i], s_ref[pl.ds(at + i, 1), :]) for i in range(g)]
            for i in range(g):
                to = to_ref[at + i] - base
                blk = to // n1
                apart = jnp.where(blk % 2 == side, 0, half)
                acc_ref[apart + (blk // 2) * n1 + (to - blk * n1)] += pieces[i]
            return carry

        lax.fori_loop(0, steps, step, 0)
        own_ref[...] = acc_ref[:half]
        pair = lax.axis_index("blk") // 2
        for q in range(pairs):
            at = pl.ds(half + (pair + pairs - 1 - q) % pairs * n1, n1)
            place = q % cut * n1
            others[q // cut][place : place + n1] = acc_ref[at].astype(BF16)

    return pl.pallas_call(
        kernel,
        in_specs=[SMEM] * 2 + [VMEM] * (parts + 4),
        out_specs=[VMEM] * 5,
        out_shape=[
            sds(rhs.shape, F32),
            sds((half, r, vb), F32),
            sds((cut * n1, r, vb), BF16),
            sds(((pairs - cut) * n1, r, vb), BF16),
            sds((n + map_rows, vb), jnp.int32),
        ],
        scratch_shapes=[pltpu.VMEM((3 * n, r, vb), BF16), pltpu.VMEM((2 * half, r, vb), F32)],
        compiler_params=params(16),
        cost_estimate=cost(n * 0.15),
    )(cols, to_mid, *x_parts, pack, rhs, slots, map_row)


def pair_sums(own, got, last, n1):
    half, r, vb = own.shape
    count = got.shape[0] // n1

    def kernel(own_ref, got_ref, *refs):
        pair = lax.axis_index("blk") // 2
        for k in range(count):
            at = pl.ds((pair + last - k) % (half // n1) * n1, n1)
            total = own_ref[at] + got_ref[k * n1 : (k + 1) * n1].astype(F32)
            refs[k][...] = total.astype(BF16)

    return pl.pallas_call(
        kernel,
        in_specs=[VMEM] * 2,
        out_specs=[VMEM] * count,
        out_shape=[sds((n1, r, vb), BF16)] * count,
        compiler_params=params(12),
        cost_estimate=cost(0.2),
    )(own, got)


def fine_last(cols, to_mid, slots, tables, mid_parts, pack, resid, fields, others):
    n, r, vb = resid.shape
    g = in_groups(fields[0].shape[0])
    steps = n // g
    wide = next(w for w in (16, 12, 8, 6, 4, 3, 2, 1) if n % w == 0)
    parts = len(mid_parts)
    half = parts // 2
    n1 = mid_parts[0].shape[0]

    def kernel(cols_ref, to_ref, near_to_ref, far_to_ref, s_ref, near_ref, far_ref, *refs):
        mid_refs, (pack_ref, z_ref), refs = refs[:parts], refs[parts : parts + 2], refs[parts + 2 :]
        v_refs, refs = refs[: len(fields)], refs[len(fields) :]
        other_refs, (out_hbm, *other_hbm), (f_ref, x_ref, all_ref, sems, other_sems) = (
            refs[: len(others)],
            refs[len(others) : 2 * len(others) + 1],
            refs[2 * len(others) + 1 :],
        )
        other_copies = [
            pltpu.make_async_copy(source, dest, other_sems.at[q])
            for q, (source, dest) in enumerate(zip(other_refs, other_hbm))
        ]
        for copy in other_copies:
            copy.start()

        def out_copy(j):
            at = pl.ds(j * g, g)
            return pltpu.make_async_copy(f_ref.at[at], out_hbm.at[at], sems.at[j])

        blk = lax.axis_index("blk")
        side = blk % 2
        base = lax.axis_index("fold") * (parts * n1)
        for p in range(parts):
            owner = (blk // 2 + half - p % half) % half * 2 + (side if p < half else 1 - side)
            all_ref[pl.ds(owner * n1, n1)] = mid_refs[parts - 1 - p][...].astype(F32)

        def lift(start, slots_of, to_of):
            def some(j, carry):
                lifted = []
                for q in range(wide):
                    index = jnp.broadcast_to(slots_of[pl.ds(j * wide + q, 1), :], (r, vb))
                    h = all_ref[to_of(j * wide + q) - base]
                    lifted.append(jnp.take_along_axis(h, index, axis=1))
                for q in range(wide):
                    x_ref[start + j * wide + q] = lifted[q].astype(BF16)
                return carry

            lax.fori_loop(0, n // wide, some, 0)

        def from_table(ref):
            if n <= vb:
                return lambda i: ref[n, i]
            return lambda i: ref[n + i // vb, i % vb]

        lift(n, s_ref, lambda i: to_ref[i])
        lift((1 - side) * (2 * n), near_ref, from_table(near_to_ref))
        lift(side * (2 * n), far_ref, from_table(far_to_ref))
        ring = first_before(n, True)

        def step(j, v_ref, low):
            at = j * g
            zs = [
                z_ref[at + i] - packed_product(cols_ref, at + i, ring, x_ref, pack_ref)
                for i in range(g)
            ]
            vs = [smoothed(zs[i], pack_ref, at + i) for i in range(g)]
            for i in range(g):
                f_ref[at + i] = vs[i] + (v_ref[at - low + i] + x_ref[n + at + i].astype(F32))
            out_copy(j).start()

        low = 0
        for v_ref in v_refs:
            high = low + v_ref.shape[0]

            def some_rows(j, carry, v_ref=v_ref, low=low):
                step(j, v_ref, low)
                return carry

            lax.fori_loop(low // g, high // g, some_rows, 0)
            low = high
        for j in range(steps):
            out_copy(j).wait()
        for copy in other_copies:
            copy.wait()

    return pl.pallas_call(
        kernel,
        in_specs=[SMEM] * 4 + [VMEM] * (5 + parts + len(fields) + len(others)),
        out_specs=[ANY] * (1 + len(others)),
        out_shape=[sds(resid.shape, F32)] + [sds(a.shape, a.dtype) for a in others],
        scratch_shapes=[
            pltpu.VMEM((n, r, vb), F32),
            pltpu.VMEM((3 * n, r, vb), BF16),
            pltpu.VMEM((parts * n1, r, vb), F32),
            pltpu.SemaphoreType.DMA((steps,)),
            pltpu.SemaphoreType.DMA((len(others),)),
        ],
        compiler_params=params(16),
        cost_estimate=cost(n * 0.2),
    )(
        cols,
        to_mid,
        *tables,
        slots,
        *tables,
        *mid_parts[::-1],
        pack,
        resid,
        *fields,
        *others,
    )


def packed(tiles, smoother, after):
    n, kt, vb, _ = tiles.shape

    def kernel(t_ref, m_ref, after_ref, o_ref):
        def one(i, carry):
            for k in range(kt):
                o_ref[i, k] = t_ref[i, k].T
            o_ref[i, kt] = m_ref[i].T
            return carry

        lax.fori_loop(0, n, one, 0)

    return pl.pallas_call(
        kernel,
        in_specs=[VMEM] * 2 + [ANY],
        out_specs=VMEM,
        out_shape=sds((n, kt + 1, vb, vb), BF16),
        compiler_params=params(12),
        cost_estimate=cost(2),
    )(tiles, smoother, after)


def add_and_smooth(pack, terms):
    shape = terms[0].shape

    def kernel(pack_ref, *refs):
        term_refs, (rhs_ref, f_ref, h_ref) = refs[:-3], refs[-3:]
        totals = []
        for i in range(shape[0]):
            total = term_refs[0][i].astype(F32)
            for t in term_refs[1:]:
                total = total + t[i].astype(F32)
            totals.append(total)
        vs = [smoothed(total, pack_ref, i) for i, total in enumerate(totals)]
        for i, v in enumerate(vs):
            rhs_ref[i] = totals[i]
            f_ref[i] = v
            h_ref[i] = v.astype(BF16)

    return pl.pallas_call(
        kernel,
        in_specs=[VMEM] * (1 + len(terms)),
        out_specs=[VMEM] * 3,
        out_shape=[sds(shape, F32), sds(shape, F32), sds(shape, BF16)],
        compiler_params=params(12),
        cost_estimate=cost(0.3),
    )(pack, *terms)


def small_sweep(folded, cols, x3, pack, rhs, field, last=False):
    n, r, vb = rhs.shape
    pick = BF16 if r % 16 == 0 else F32
    kinds = [BF16] if last else [BF16, F32]

    def kernel(cols_ref, c_ref, b_ref, a_ref, pack_ref, rhs_ref, v_ref, *refs):
        out_refs, x_ref = refs[:-1], refs[-1]
        fill(x_ref, (a_ref, b_ref, c_ref))
        ring = first_before(n, folded)
        zs = [rhs_ref[i] - packed_product(cols_ref, i, ring, x_ref, pack_ref) for i in range(n)]
        vs = [v_ref[i] + smoothed(zs[i], pack_ref, i) for i in range(n)]
        for i, v in enumerate(vs):
            for out_ref in out_refs:
                out_ref[i] = v.astype(out_ref.dtype)

    return pl.pallas_call(
        kernel,
        in_specs=[SMEM] + [VMEM] * 6,
        out_specs=[VMEM] * len(kinds),
        out_shape=[sds(rhs.shape, kind) for kind in kinds],
        scratch_shapes=[pltpu.VMEM((3 * n, r, vb), pick)],
        compiler_params=params(12),
        cost_estimate=cost(1),
    )(cols, *x3[::-1], pack, rhs, field)


def mid_restrict(cols, to_low, x3, pack, rhs, slots, lows):
    n, r, vb = rhs.shape
    folds = lax.axis_size("fold")
    share = r // folds

    def kernel(cols_ref, to_ref, c_ref, b_ref, a_ref, pack_ref, rhs_ref, s_ref, *refs):
        outs, (x_ref, acc_ref, cut_ref) = refs[:folds], refs[folds:]
        fill(x_ref, (a_ref, b_ref, c_ref))
        acc_ref[...] = jnp.zeros_like(acc_ref)
        ring = first_before(n, True)
        zs = [rhs_ref[i] - packed_product(cols_ref, i, ring, x_ref, pack_ref) for i in range(n)]
        pieces = [collected(zs[i], s_ref[i : i + 1, :]) for i in range(n)]
        base = lax.axis_index("blk") * lows
        for i in range(n):
            acc_ref[to_ref[i] - base] += pieces[i]
        for f in range(folds):
            cut_ref[f] = acc_ref[:, f * share : (f + 1) * share, :]
        for f in range(folds):
            outs[f][...] = cut_ref[(lax.axis_index("fold") + f) % folds].astype(BF16)

    return pl.pallas_call(
        kernel,
        in_specs=[SMEM] * 2 + [VMEM] * 6,
        out_specs=[VMEM] * folds,
        out_shape=[sds((lows, share, vb), BF16)] * folds,
        scratch_shapes=[
            pltpu.VMEM((3 * n, r, vb), BF16),
            pltpu.VMEM((lows, r, vb), F32),
            pltpu.VMEM((folds, lows, share, vb), F32),
        ],
        compiler_params=params(12),
    )(cols, to_low, *x3[::-1], pack, rhs, slots)


def mid_lift(to_low, parts, field, slots):
    n, r, vb = field.shape
    folds = len(parts)
    lows, share = parts[0].shape[:2]

    def kernel(to_ref, *refs):
        part_refs, (v_ref, s_ref, c_ref, f_ref, h_ref, cut_ref) = refs[:folds], refs[folds:]
        for f in range(folds):
            owner = (lax.axis_index("fold") + folds - f) % folds
            cut_ref[owner] = part_refs[f][...].astype(F32)
        for f in range(folds):
            c_ref[:, f * share : (f + 1) * share, :] = cut_ref[f]
        for i in range(n):
            index = jnp.broadcast_to(s_ref[i : i + 1, :], (r, vb))
            low = to_ref[i] - lax.axis_index("blk") * lows
            v = v_ref[i] + jnp.take_along_axis(c_ref[low], index, axis=1)
            f_ref[i] = v
            h_ref[i] = v.astype(BF16)

    return pl.pallas_call(
        kernel,
        in_specs=[SMEM] + [VMEM] * (folds + 2),
        out_specs=[VMEM] * 3,
        out_shape=[sds((lows, r, vb), F32), sds(field.shape, F32), sds(field.shape, BF16)],
        scratch_shapes=[pltpu.VMEM((folds, lows, share, vb), F32)],
        compiler_params=params(16),
    )(to_low, *parts, field, slots)


def on_device(
    fine_rhs,
    fine_tiles,
    fine_cols,
    fine_smoother,
    fine_map,
    fine_slots,
    mid_tiles,
    mid_cols,
    mid_smoother,
    mid_map,
    mid_slots,
    coarse_tiles,
    coarse_cols,
    coarse_smoother,
):
    n0, r, vb = fine_rhs.shape
    n1 = mid_tiles.shape[0]
    n2 = coarse_tiles.shape[0]
    blks, folds = lax.axis_size("blk"), lax.axis_size("fold")
    pairs = blks // 2
    cols0, cols1, cols2 = fine_cols.T, mid_cols.T, coarse_cols.T

    halves, chunks = HALVES, CHUNKS
    count = n0 // halves
    v, h = [], []
    for k in range(halves):
        part, rough = fine_first(k * count, count, chunks, fine_smoother, fine_rhs)
        v.append(part)
        h += rough
    x = h + pair_halos(h)
    fine_tiles = brought(fine_tiles, x[2 * halves * chunks])
    down, h = [], []
    for k in range(halves):
        part, rough = fine_sweep(
            k * count, count, chunks, cols0, x, fine_tiles, fine_smoother, fine_rhs, v[k]
        )
        down.append(part)
        h += rough
    x = h + pair_halos(h)
    fine_pack = packed(fine_tiles, fine_smoother, x[2 * halves * chunks - 1])
    resid, own, *others, table = fine_restrict(
        cols0, fine_map, x, fine_pack, fine_rhs, fine_slots, fine_map[None], n1
    )
    steps = [[(i, (i + 2 * k) % blks) for i in range(blks)] for k in range(pairs)]
    late = partner(others[1])
    early = partner(others[0])
    early, near = lax.optimization_barrier((early, partner(table)))
    mid_pack = packed(mid_tiles, mid_smoother, others[0])
    low_pack = packed(coarse_tiles, coarse_smoother, others[0])
    early, mid_pack, low_pack = lax.optimization_barrier((early, mid_pack, low_pack))
    cut = others[1].shape[0] // n1
    sums = pair_sums(own, early, pairs - 1, n1) + pair_sums(own, late, cut - 1, n1)
    sums = sums[::-1]
    tables = [near, forwarded(near)]
    terms = [sums[0]] + [lax.ppermute(sums[k], "blk", steps[k]) for k in range(1, pairs)]
    terms, tables = lax.optimization_barrier((terms, tables))

    mid_rhs, w, h = add_and_smooth(mid_pack, terms)
    before, after = halos(h)
    w, h = small_sweep(True, cols1, (before, h, after), mid_pack, mid_rhs, w)[::-1]
    before, after = halos(h)
    cuts = mid_restrict(cols1, mid_map, (before, h, after), mid_pack, mid_rhs, mid_slots, n2)

    shifts = [[(i, (i + k) % folds) for i in range(folds)] for k in range(folds)]
    terms = [cuts[0]] + [lax.ppermute(cuts[k], "fold", shifts[k]) for k in range(1, folds)]
    low_rhs, c, h = add_and_smooth(low_pack, terms)
    for k in range(1, COARSE):
        before, after = halos(h)
        h, *c = small_sweep(
            False, cols2, (before, h, after), low_pack, low_rhs, c, last=k == COARSE - 1
        )
        c = c[0] if c else None
    parts = [h] + [lax.ppermute(h, "fold", shifts[k]) for k in range(1, folds)]

    coarse_field, w, h = mid_lift(mid_map, parts, w, mid_slots)
    before, after = halos(h)
    h, mid_field = small_sweep(True, cols1, (before, h, after), mid_pack, mid_rhs, w)

    far_mids = [lax.ppermute(h, "blk", steps[k]) for k in range(pairs - 1, 0, -1)]
    mids = [h] + far_mids[::-1]
    mids = mids + [partner(m) for m in far_mids + [h]][::-1]
    fine_field, mid_field, coarse_field = fine_last(
        cols0,
        fine_map,
        fine_slots,
        tables,
        mids,
        fine_pack,
        resid,
        down,
        (mid_field, coarse_field),
    )
    return fine_field, mid_field, coarse_field


def solution(mesh):
    both = ("fold", "blk")
    return jax.shard_map(
        on_device,
        mesh=mesh,
        in_specs=(
            P(both, None, None),
            P(both, None, None, None),
            P(both, None),
            P(both, None, None),
            P(both),
            P(both, None),
            P(both, None, None, None),
            P(both, None),
            P(both, None, None),
            P(both),
            P(both, None),
            P("blk", None, None, None),
            P("blk", None),
            P("blk", None, None),
        ),
        out_specs=(P(both, None, None), P(both, None, None), P("blk", None, None)),
        check_vma=False,
    )
```

```python
import jax
import jax.numpy as jnp
from jax import lax
from jax.experimental import pallas as pl
from jax.experimental.pallas import tpu as pltpu
from jax.sharding import PartitionSpec as P

COARSE = 8
HALVES, CHUNKS = 2, 2
F32 = jnp.float32
BF16 = jnp.bfloat16
NT = (((1,), (1,)), ((), ()))
NN = (((1,), (0,)), ((), ()))
ANY = pl.BlockSpec(memory_space=pl.ANY)
VMEM = pl.BlockSpec(memory_space=pltpu.VMEM)
SMEM = pl.BlockSpec(memory_space=pltpu.SMEM)
MIB = 1 << 20


def sds(shape, dtype):
    return jax.ShapeDtypeStruct(shape, dtype)


def params(mib):
    return pltpu.CompilerParams(vmem_limit_bytes=mib * MIB)


def times(x, tile):
    return lax.dot_general(x, tile, NT, preferred_element_type=F32)


def first_before(per, folded):
    blks = lax.axis_size("blk")
    blk = lax.axis_index("blk")
    base = lax.axis_index("fold") * (blks * per) if folded else 0
    return base + (blk - 1) * per, blks * per


def picked(cols_ref, row, ring, x_ref):
    first, total = ring
    blocks = []
    for k in range(cols_ref.shape[0]):
        place = cols_ref[k, row] - first
        place = jnp.where(place < 0, place + total, place)
        place = jnp.where(place >= total, place - total, place)
        blocks.append(x_ref[place])
    return jnp.concatenate(blocks, axis=1).astype(BF16)


def row_product(cols_ref, row, ring, x_ref, tiles_ref):
    t = jnp.concatenate([tiles_ref[row, k] for k in range(tiles_ref.shape[1])], axis=1)
    return times(picked(cols_ref, row, ring, x_ref), t)


def packed_product(cols_ref, row, ring, x_ref, pack_ref):
    kt, vb = pack_ref.shape[1] - 1, pack_ref.shape[2]
    t = pack_ref[row, :kt].reshape(kt * vb, vb)
    x = picked(cols_ref, row, ring, x_ref)
    return lax.dot_general(x, t, NN, preferred_element_type=F32)


def smoothed(z, pack_ref, row):
    last = pack_ref.shape[1] - 1
    return lax.dot_general(z.astype(BF16), pack_ref[row, last], NN, preferred_element_type=F32)


def fill(dest, parts, at=0):
    for part in parts:
        dest[pl.ds(at, part.shape[0])] = part[...].astype(dest.dtype)
        at = at + part.shape[0]


def fill_pair(dest, parts, n):
    side = lax.axis_index("blk") % 2
    third = len(parts) // 3
    fill(dest, parts[:third], n)
    fill(dest, parts[third : 2 * third], (1 - side) * (2 * n))
    fill(dest, parts[2 * third :], side * (2 * n))


def in_groups(count):
    return next(g for g in (12, 8, 6, 4, 3, 2, 1) if count % g == 0)


def cost(us):
    return pl.CostEstimate(flops=0, bytes_accessed=int(us * 3.0e6), transcendentals=0)


def halos(value):
    n = lax.axis_size("blk")
    up = [(i, (i + 1) % n) for i in range(n)]
    down = [((i + 1) % n, i) for i in range(n)]
    return lax.ppermute(value, "blk", up), lax.ppermute(value, "blk", down)


def partner(value):
    n = lax.axis_size("blk")
    return lax.ppermute(value, "blk", [(i, i ^ 1) for i in range(n)])


def forwarded(value):
    n = lax.axis_size("blk")
    return lax.ppermute(value, "blk", [(i, (i + 2 - 4 * (i % 2)) % n) for i in range(n)])


def pair_halos(chunks):
    near = [partner(c) for c in chunks]
    return near + [forwarded(c) for c in near]


def store_chunks(i, value, h_refs):
    size = h_refs[0].shape[0]
    for c, h_ref in enumerate(h_refs):

        @pl.when((i >= c * size) & (i < (c + 1) * size))
        def _(c=c, h_ref=h_ref):
            h_ref[pl.ds(i - c * size, value.shape[0])] = value


def fine_first(low, count, chunks, smoother, rhs):
    n, r, vb = rhs.shape
    size = count // chunks
    g = in_groups(size)
    steps = count // g

    def kernel(m_ref, rhs_ref, f_ref, *h_refs):
        def step(j, carry):
            at = j * g
            vs = [
                times(rhs_ref[low + at + i].astype(BF16), m_ref[low + at + i]) for i in range(g)
            ]
            for i in range(g):
                f_ref[at + i] = vs[i]
            store_chunks(at, jnp.stack([v.astype(BF16) for v in vs]), h_refs)
            return carry

        lax.fori_loop(0, steps, step, 0)

    f, *h = pl.pallas_call(
        kernel,
        in_specs=[VMEM] * 2,
        out_specs=[VMEM] * (1 + chunks),
        out_shape=[sds((count, r, vb), F32)] + [sds((size, r, vb), BF16)] * chunks,
        compiler_params=params(12),
        cost_estimate=cost(count * 0.04),
    )(smoother, rhs)
    return f, h


def brought(source, after):
    n = source.shape[0]
    parts = in_groups(n)
    size = n // parts

    def kernel(source_ref, after_ref, copied_ref, sems):
        copies = []
        for p in range(parts):
            at = pl.ds(p * size, size)
            copies.append(pltpu.make_async_copy(source_ref.at[at], copied_ref.at[at], sems.at[p]))
        for copy in copies:
            copy.start()
        for copy in copies:
            copy.wait()

    return pl.pallas_call(
        kernel,
        in_specs=[ANY] * 2,
        out_specs=VMEM,
        out_shape=sds(source.shape, source.dtype),
        scratch_shapes=[pltpu.SemaphoreType.DMA((parts,))],
        compiler_params=params(12),
        cost_estimate=cost(3),
    )(source, after)


def fine_sweep(low, count, chunks, cols, x_parts, tiles, smoother, rhs, field):
    n, r, vb = rhs.shape
    size = count // chunks
    g = in_groups(size)
    steps = count // g
    parts = len(x_parts)

    def kernel(cols_ref, *refs):
        x_refs, (t_ref, m_ref, rhs_ref, v_ref, f_ref), (*h_refs, x_ref) = (
            refs[:parts],
            refs[parts : parts + 5],
            refs[parts + 5 :],
        )
        fill_pair(x_ref, x_refs, n)
        ring = first_before(n, True)

        def step(j, carry):
            at = j * g
            zs = []
            for i in range(g):
                row = low + at + i
                z = rhs_ref[row] - row_product(cols_ref, row, ring, x_ref, t_ref)
                zs.append(z.astype(BF16))
            vs = [v_ref[at + i] + times(zs[i], m_ref[low + at + i]) for i in range(g)]
            for i in range(g):
                f_ref[at + i] = vs[i]
            store_chunks(at, jnp.stack([v.astype(BF16) for v in vs]), h_refs)
            return carry

        lax.fori_loop(0, steps, step, 0)

    f, *h = pl.pallas_call(
        kernel,
        in_specs=[SMEM] + [VMEM] * (parts + 4),
        out_specs=[VMEM] * (1 + chunks),
        out_shape=[sds((count, r, vb), F32)] + [sds((size, r, vb), BF16)] * chunks,
        scratch_shapes=[pltpu.VMEM((3 * n, r, vb), BF16)],
        compiler_params=params(12),
        cost_estimate=cost(count * 0.15),
    )(cols, *x_parts, tiles, smoother, rhs, field)
    return f, h


def one_hot(slots_row, vb):
    return (lax.broadcasted_iota(jnp.int32, (vb, vb), 0) == slots_row).astype(F32).astype(BF16)


def collected(z, slots_row):
    r, vb = z.shape
    high = z.astype(BF16)
    low = (z - high.astype(F32)).astype(BF16)
    both = times(jnp.concatenate([high, low], axis=0), one_hot(slots_row, vb))
    return both[:r] + both[r:]


def fine_restrict(cols, to_mid, x_parts, pack, rhs, slots, map_row, n1):
    n, r, vb = rhs.shape
    g = in_groups(n)
    steps = n // g
    parts = len(x_parts)
    blks = lax.axis_size("blk")
    pairs = blks // 2
    half = pairs * n1
    map_rows = -(-n // vb)
    cut = (pairs + 1) // 2

    def kernel(cols_ref, to_ref, *refs):
        x_refs, refs = refs[:parts], refs[parts:]
        pack_ref, rhs_ref, s_ref, map_ref, z_ref, own_ref, *others, table_ref, x_ref, acc_ref = refs
        fill_pair(x_ref, x_refs, n)
        acc_ref[...] = jnp.zeros_like(acc_ref)
        table_ref[:n] = s_ref[...]
        for q in range(map_rows):
            size = min(vb, n - q * vb)
            table_ref[n + q : n + q + 1, :size] = map_ref[:, q * vb : q * vb + size]
        ring = first_before(n, True)
        side = lax.axis_index("blk") % 2
        base = lax.axis_index("fold") * (blks * n1)

        def step(j, carry):
            at = j * g
            zs = [
                rhs_ref[at + i] - packed_product(cols_ref, at + i, ring, x_ref, pack_ref)
                for i in range(g)
            ]
            for i in range(g):
                z_ref[at + i] = zs[i]
            pieces = [collected(zs[i], s_ref[pl.ds(at + i, 1), :]) for i in range(g)]
            for i in range(g):
                to = to_ref[at + i] - base
                blk = to // n1
                apart = jnp.where(blk % 2 == side, 0, half)
                acc_ref[apart + (blk // 2) * n1 + (to - blk * n1)] += pieces[i]
            return carry

        lax.fori_loop(0, steps, step, 0)
        own_ref[...] = acc_ref[:half]
        pair = lax.axis_index("blk") // 2
        for q in range(pairs):
            at = pl.ds(half + (pair + pairs - 1 - q) % pairs * n1, n1)
            place = q % cut * n1
            others[q // cut][place : place + n1] = acc_ref[at].astype(BF16)

    return pl.pallas_call(
        kernel,
        in_specs=[SMEM] * 2 + [VMEM] * (parts + 4),
        out_specs=[VMEM] * 5,
        out_shape=[
            sds(rhs.shape, F32),
            sds((half, r, vb), F32),
            sds((cut * n1, r, vb), BF16),
            sds(((pairs - cut) * n1, r, vb), BF16),
            sds((n + map_rows, vb), jnp.int32),
        ],
        scratch_shapes=[pltpu.VMEM((3 * n, r, vb), BF16), pltpu.VMEM((2 * half, r, vb), F32)],
        compiler_params=params(16),
        cost_estimate=cost(n * 0.15),
    )(cols, to_mid, *x_parts, pack, rhs, slots, map_row)


def pair_sums(own, got, last, n1):
    half, r, vb = own.shape
    count = got.shape[0] // n1

    def kernel(own_ref, got_ref, *refs):
        pair = lax.axis_index("blk") // 2
        for k in range(count):
            at = pl.ds((pair + last - k) % (half // n1) * n1, n1)
            total = own_ref[at] + got_ref[k * n1 : (k + 1) * n1].astype(F32)
            refs[k][...] = total.astype(BF16)

    return pl.pallas_call(
        kernel,
        in_specs=[VMEM] * 2,
        out_specs=[VMEM] * count,
        out_shape=[sds((n1, r, vb), BF16)] * count,
        compiler_params=params(12),
        cost_estimate=cost(0.2),
    )(own, got)


def fine_last(cols, to_mid, slots, tables, mid_parts, pack, resid, fields, others):
    n, r, vb = resid.shape
    g = in_groups(fields[0].shape[0])
    steps = n // g
    wide = next(w for w in (16, 12, 8, 6, 4, 3, 2, 1) if n % w == 0)
    parts = len(mid_parts)
    half = parts // 2
    n1 = mid_parts[0].shape[0]

    def kernel(cols_ref, to_ref, near_to_ref, far_to_ref, s_ref, near_ref, far_ref, *refs):
        mid_refs, (pack_ref, z_ref), refs = refs[:parts], refs[parts : parts + 2], refs[parts + 2 :]
        v_refs, refs = refs[: len(fields)], refs[len(fields) :]
        other_refs, (out_hbm, *other_hbm), (f_ref, x_ref, all_ref, sems, other_sems) = (
            refs[: len(others)],
            refs[len(others) : 2 * len(others) + 1],
            refs[2 * len(others) + 1 :],
        )
        other_copies = [
            pltpu.make_async_copy(source, dest, other_sems.at[q])
            for q, (source, dest) in enumerate(zip(other_refs, other_hbm))
        ]
        for copy in other_copies:
            copy.start()

        def out_copy(j):
            at = pl.ds(j * g, g)
            return pltpu.make_async_copy(f_ref.at[at], out_hbm.at[at], sems.at[j])

        blk = lax.axis_index("blk")
        side = blk % 2
        base = lax.axis_index("fold") * (parts * n1)
        for p in range(parts):
            owner = (blk // 2 + half - p % half) % half * 2 + (side if p < half else 1 - side)
            all_ref[pl.ds(owner * n1, n1)] = mid_refs[parts - 1 - p][...].astype(F32)

        def lift(start, slots_of, to_of):
            def some(j, carry):
                lifted = []
                for q in range(wide):
                    index = jnp.broadcast_to(slots_of[pl.ds(j * wide + q, 1), :], (r, vb))
                    h = all_ref[to_of(j * wide + q) - base]
                    lifted.append(jnp.take_along_axis(h, index, axis=1))
                for q in range(wide):
                    x_ref[start + j * wide + q] = lifted[q].astype(BF16)
                return carry

            lax.fori_loop(0, n // wide, some, 0)

        def from_table(ref):
            if n <= vb:
                return lambda i: ref[n, i]
            return lambda i: ref[n + i // vb, i % vb]

        lift(n, s_ref, lambda i: to_ref[i])
        lift((1 - side) * (2 * n), near_ref, from_table(near_to_ref))
        lift(side * (2 * n), far_ref, from_table(far_to_ref))
        ring = first_before(n, True)

        def step(j, v_ref, low):
            at = j * g
            zs = [
                z_ref[at + i] - packed_product(cols_ref, at + i, ring, x_ref, pack_ref)
                for i in range(g)
            ]
            vs = [smoothed(zs[i], pack_ref, at + i) for i in range(g)]
            for i in range(g):
                f_ref[at + i] = vs[i] + (v_ref[at - low + i] + x_ref[n + at + i].astype(F32))
            out_copy(j).start()

        low = 0
        for v_ref in v_refs:
            high = low + v_ref.shape[0]

            def some_rows(j, carry, v_ref=v_ref, low=low):
                step(j, v_ref, low)
                return carry

            lax.fori_loop(low // g, high // g, some_rows, 0)
            low = high
        for j in range(steps):
            out_copy(j).wait()
        for copy in other_copies:
            copy.wait()

    return pl.pallas_call(
        kernel,
        in_specs=[SMEM] * 4 + [VMEM] * (5 + parts + len(fields) + len(others)),
        out_specs=[ANY] * (1 + len(others)),
        out_shape=[sds(resid.shape, F32)] + [sds(a.shape, a.dtype) for a in others],
        scratch_shapes=[
            pltpu.VMEM((n, r, vb), F32),
            pltpu.VMEM((3 * n, r, vb), BF16),
            pltpu.VMEM((parts * n1, r, vb), F32),
            pltpu.SemaphoreType.DMA((steps,)),
            pltpu.SemaphoreType.DMA((len(others),)),
        ],
        compiler_params=params(16),
        cost_estimate=cost(n * 0.2),
    )(
        cols,
        to_mid,
        *tables,
        slots,
        *tables,
        *mid_parts[::-1],
        pack,
        resid,
        *fields,
        *others,
    )


def packed(tiles, smoother, after):
    n, kt, vb, _ = tiles.shape

    def kernel(t_ref, m_ref, after_ref, o_ref):
        def one(i, carry):
            for k in range(kt):
                o_ref[i, k] = t_ref[i, k].T
            o_ref[i, kt] = m_ref[i].T
            return carry

        lax.fori_loop(0, n, one, 0)

    return pl.pallas_call(
        kernel,
        in_specs=[VMEM] * 2 + [ANY],
        out_specs=VMEM,
        out_shape=sds((n, kt + 1, vb, vb), BF16),
        compiler_params=params(12),
        cost_estimate=cost(2),
    )(tiles, smoother, after)


def add_and_smooth(pack, terms):
    shape = terms[0].shape

    def kernel(pack_ref, *refs):
        term_refs, (rhs_ref, f_ref, h_ref) = refs[:-3], refs[-3:]
        totals = []
        for i in range(shape[0]):
            total = term_refs[0][i].astype(F32)
            for t in term_refs[1:]:
                total = total + t[i].astype(F32)
            totals.append(total)
        vs = [smoothed(total, pack_ref, i) for i, total in enumerate(totals)]
        for i, v in enumerate(vs):
            rhs_ref[i] = totals[i]
            f_ref[i] = v
            h_ref[i] = v.astype(BF16)

    return pl.pallas_call(
        kernel,
        in_specs=[VMEM] * (1 + len(terms)),
        out_specs=[VMEM] * 3,
        out_shape=[sds(shape, F32), sds(shape, F32), sds(shape, BF16)],
        compiler_params=params(12),
        cost_estimate=cost(0.3),
    )(pack, *terms)


def small_sweep(folded, cols, x3, pack, rhs, field, last=False):
    n, r, vb = rhs.shape
    pick = BF16 if r % 16 == 0 else F32
    kinds = [BF16] if last else [BF16, F32]

    def kernel(cols_ref, c_ref, b_ref, a_ref, pack_ref, rhs_ref, v_ref, *refs):
        out_refs, x_ref = refs[:-1], refs[-1]
        fill(x_ref, (a_ref, b_ref, c_ref))
        ring = first_before(n, folded)
        zs = [rhs_ref[i] - packed_product(cols_ref, i, ring, x_ref, pack_ref) for i in range(n)]
        vs = [v_ref[i] + smoothed(zs[i], pack_ref, i) for i in range(n)]
        for i, v in enumerate(vs):
            for out_ref in out_refs:
                out_ref[i] = v.astype(out_ref.dtype)

    return pl.pallas_call(
        kernel,
        in_specs=[SMEM] + [VMEM] * 6,
        out_specs=[VMEM] * len(kinds),
        out_shape=[sds(rhs.shape, kind) for kind in kinds],
        scratch_shapes=[pltpu.VMEM((3 * n, r, vb), pick)],
        compiler_params=params(12),
        cost_estimate=cost(1),
    )(cols, *x3[::-1], pack, rhs, field)


def mid_restrict(cols, to_low, x3, pack, rhs, slots, lows):
    n, r, vb = rhs.shape
    folds = lax.axis_size("fold")
    share = r // folds

    def kernel(cols_ref, to_ref, c_ref, b_ref, a_ref, pack_ref, rhs_ref, s_ref, *refs):
        outs, (x_ref, acc_ref, cut_ref) = refs[:folds], refs[folds:]
        fill(x_ref, (a_ref, b_ref, c_ref))
        acc_ref[...] = jnp.zeros_like(acc_ref)
        ring = first_before(n, True)
        zs = [rhs_ref[i] - packed_product(cols_ref, i, ring, x_ref, pack_ref) for i in range(n)]
        pieces = [collected(zs[i], s_ref[i : i + 1, :]) for i in range(n)]
        base = lax.axis_index("blk") * lows
        for i in range(n):
            acc_ref[to_ref[i] - base] += pieces[i]
        for f in range(folds):
            cut_ref[f] = acc_ref[:, f * share : (f + 1) * share, :]
        for f in range(folds):
            outs[f][...] = cut_ref[(lax.axis_index("fold") + f) % folds].astype(BF16)

    return pl.pallas_call(
        kernel,
        in_specs=[SMEM] * 2 + [VMEM] * 6,
        out_specs=[VMEM] * folds,
        out_shape=[sds((lows, share, vb), BF16)] * folds,
        scratch_shapes=[
            pltpu.VMEM((3 * n, r, vb), BF16),
            pltpu.VMEM((lows, r, vb), F32),
            pltpu.VMEM((folds, lows, share, vb), F32),
        ],
        compiler_params=params(12),
    )(cols, to_low, *x3[::-1], pack, rhs, slots)


def mid_lift(to_low, parts, field, slots):
    n, r, vb = field.shape
    folds = len(parts)
    lows, share = parts[0].shape[:2]

    def kernel(to_ref, *refs):
        part_refs, (v_ref, s_ref, c_ref, f_ref, h_ref, cut_ref) = refs[:folds], refs[folds:]
        for f in range(folds):
            owner = (lax.axis_index("fold") + folds - f) % folds
            cut_ref[owner] = part_refs[f][...].astype(F32)
        for f in range(folds):
            c_ref[:, f * share : (f + 1) * share, :] = cut_ref[f]
        for i in range(n):
            index = jnp.broadcast_to(s_ref[i : i + 1, :], (r, vb))
            low = to_ref[i] - lax.axis_index("blk") * lows
            v = v_ref[i] + jnp.take_along_axis(c_ref[low], index, axis=1)
            f_ref[i] = v
            h_ref[i] = v.astype(BF16)

    return pl.pallas_call(
        kernel,
        in_specs=[SMEM] + [VMEM] * (folds + 2),
        out_specs=[VMEM] * 3,
        out_shape=[sds((lows, r, vb), F32), sds(field.shape, F32), sds(field.shape, BF16)],
        scratch_shapes=[pltpu.VMEM((folds, lows, share, vb), F32)],
        compiler_params=params(16),
    )(to_low, *parts, field, slots)


def on_device(
    fine_rhs,
    fine_tiles,
    fine_cols,
    fine_smoother,
    fine_map,
    fine_slots,
    mid_tiles,
    mid_cols,
    mid_smoother,
    mid_map,
    mid_slots,
    coarse_tiles,
    coarse_cols,
    coarse_smoother,
):
    n0, r, vb = fine_rhs.shape
    n1 = mid_tiles.shape[0]
    n2 = coarse_tiles.shape[0]
    blks, folds = lax.axis_size("blk"), lax.axis_size("fold")
    pairs = blks // 2
    cols0, cols1, cols2 = fine_cols.T, mid_cols.T, coarse_cols.T

    halves, chunks = HALVES, CHUNKS
    count = n0 // halves
    v, h = [], []
    for k in range(halves):
        part, rough = fine_first(k * count, count, chunks, fine_smoother, fine_rhs)
        v.append(part)
        h += rough
    x = h + pair_halos(h)
    fine_tiles = brought(fine_tiles, x[2 * halves * chunks])
    down, h = [], []
    for k in range(halves):
        part, rough = fine_sweep(
            k * count, count, chunks, cols0, x, fine_tiles, fine_smoother, fine_rhs, v[k]
        )
        down.append(part)
        h += rough
    x = h + pair_halos(h)
    fine_pack = packed(fine_tiles, fine_smoother, x[2 * halves * chunks - 1])
    resid, own, *others, table = fine_restrict(
        cols0, fine_map, x, fine_pack, fine_rhs, fine_slots, fine_map[None], n1
    )
    steps = [[(i, (i + 2 * k) % blks) for i in range(blks)] for k in range(pairs)]
    late = partner(others[1])
    early = partner(others[0])
    early, near = lax.optimization_barrier((early, partner(table)))
    mid_pack = packed(mid_tiles, mid_smoother, others[0])
    low_pack = packed(coarse_tiles, coarse_smoother, others[0])
    early, mid_pack, low_pack = lax.optimization_barrier((early, mid_pack, low_pack))
    cut = others[1].shape[0] // n1
    sums = pair_sums(own, early, pairs - 1, n1) + pair_sums(own, late, cut - 1, n1)
    sums = sums[::-1]
    terms = [sums[0]] + [lax.ppermute(sums[k], "blk", steps[k]) for k in range(1, pairs)]

    mid_rhs, w, h = add_and_smooth(mid_pack, terms)
    before, after = halos(h)
    w, h = small_sweep(True, cols1, (before, h, after), mid_pack, mid_rhs, w)[::-1]
    before, after = halos(h)
    cuts = mid_restrict(cols1, mid_map, (before, h, after), mid_pack, mid_rhs, mid_slots, n2)

    shifts = [[(i, (i + k) % folds) for i in range(folds)] for k in range(folds)]
    terms = [cuts[0]] + [lax.ppermute(cuts[k], "fold", shifts[k]) for k in range(1, folds)]
    terms, far = lax.optimization_barrier((terms, forwarded(near)))
    tables = [near, far]
    low_rhs, c, h = add_and_smooth(low_pack, terms)
    for k in range(1, COARSE):
        before, after = halos(h)
        h, *c = small_sweep(
            False, cols2, (before, h, after), low_pack, low_rhs, c, last=k == COARSE - 1
        )
        c = c[0] if c else None
    parts = [h] + [lax.ppermute(h, "fold", shifts[k]) for k in range(1, folds)]

    coarse_field, w, h = mid_lift(mid_map, parts, w, mid_slots)
    before, after = halos(h)
    h, mid_field = small_sweep(True, cols1, (before, h, after), mid_pack, mid_rhs, w)

    far_mids = [lax.ppermute(h, "blk", steps[k]) for k in range(pairs - 1, 0, -1)]
    mids = [h] + far_mids[::-1]
    mids = mids + [partner(m) for m in far_mids + [h]][::-1]
    fine_field, mid_field, coarse_field = fine_last(
        cols0,
        fine_map,
        fine_slots,
        tables,
        mids,
        fine_pack,
        resid,
        down,
        (mid_field, coarse_field),
    )
    return fine_field, mid_field, coarse_field


def solution(mesh):
    both = ("fold", "blk")
    return jax.shard_map(
        on_device,
        mesh=mesh,
        in_specs=(
            P(both, None, None),
            P(both, None, None, None),
            P(both, None),
            P(both, None, None),
            P(both),
            P(both, None),
            P(both, None, None, None),
            P(both, None),
            P(both, None, None),
            P(both),
            P(both, None),
            P("blk", None, None, None),
            P("blk", None),
            P("blk", None, None),
        ),
        out_specs=(P(both, None, None), P(both, None, None), P("blk", None, None)),
        check_vma=False,
    )
```

```python
import jax
import jax.numpy as jnp
from jax import lax
from jax.experimental import pallas as pl
from jax.experimental.pallas import tpu as pltpu
from jax.sharding import PartitionSpec as P

COARSE = 8
SPLIT = (False,)
HALVES, CHUNKS = 2, 2
F32 = jnp.float32
BF16 = jnp.bfloat16
NT = (((1,), (1,)), ((), ()))
NN = (((1,), (0,)), ((), ()))
ANY = pl.BlockSpec(memory_space=pl.ANY)
VMEM = pl.BlockSpec(memory_space=pltpu.VMEM)
SMEM = pl.BlockSpec(memory_space=pltpu.SMEM)
MIB = 1 << 20


def sds(shape, dtype):
    return jax.ShapeDtypeStruct(shape, dtype)


def params(mib):
    return pltpu.CompilerParams(vmem_limit_bytes=mib * MIB)


def times(x, tile):
    return lax.dot_general(x, tile, NT, preferred_element_type=F32)


def first_before(per, folded):
    blks = lax.axis_size("blk")
    blk = lax.axis_index("blk")
    base = lax.axis_index("fold") * (blks * per) if folded else 0
    return base + (blk - 1) * per, blks * per


def picked(cols_ref, row, ring, x_ref, skip=0):
    first, total = ring
    blocks = []
    for k in range(skip, cols_ref.shape[0]):
        place = cols_ref[k, row] - first
        place = jnp.where(place < 0, place + total, place)
        place = jnp.where(place >= total, place - total, place)
        blocks.append(x_ref[place])
    return jnp.concatenate(blocks, axis=1).astype(BF16)


def row_product(cols_ref, row, ring, x_ref, tiles_ref):
    t = jnp.concatenate([tiles_ref[row, k] for k in range(tiles_ref.shape[1])], axis=1)
    return times(picked(cols_ref, row, ring, x_ref), t)


def packed_product(cols_ref, row, ring, x_ref, pack_ref, skip=0):
    kt, vb = pack_ref.shape[1] - 1, pack_ref.shape[2]
    t = pack_ref[row, skip:kt].reshape((kt - skip) * vb, vb)
    x = picked(cols_ref, row, ring, x_ref, skip)
    return lax.dot_general(x, t, NN, preferred_element_type=F32)


def smoothed(z, pack_ref, row):
    last = pack_ref.shape[1] - 1
    return lax.dot_general(z.astype(BF16), pack_ref[row, last], NN, preferred_element_type=F32)


def fill(dest, parts, at=0):
    for part in parts:
        dest[pl.ds(at, part.shape[0])] = part[...].astype(dest.dtype)
        at = at + part.shape[0]


def fill_pair(dest, parts, n):
    side = lax.axis_index("blk") % 2
    third = len(parts) // 3
    fill(dest, parts[:third], n)
    fill(dest, parts[third : 2 * third], (1 - side) * (2 * n))
    fill(dest, parts[2 * third :], side * (2 * n))


def in_groups(count):
    return next(g for g in (12, 8, 6, 4, 3, 2, 1) if count % g == 0)


def cost(us):
    return pl.CostEstimate(flops=0, bytes_accessed=int(us * 3.0e6), transcendentals=0)


def halos(value):
    n = lax.axis_size("blk")
    up = [(i, (i + 1) % n) for i in range(n)]
    down = [((i + 1) % n, i) for i in range(n)]
    return lax.ppermute(value, "blk", up), lax.ppermute(value, "blk", down)


def partner(value):
    n = lax.axis_size("blk")
    return lax.ppermute(value, "blk", [(i, i ^ 1) for i in range(n)])


def forwarded(value):
    n = lax.axis_size("blk")
    return lax.ppermute(value, "blk", [(i, (i + 2 - 4 * (i % 2)) % n) for i in range(n)])


def pair_halos(chunks):
    near = [partner(c) for c in chunks]
    return near + [forwarded(c) for c in near]


def store_chunks(i, value, h_refs):
    size = h_refs[0].shape[0]
    for c, h_ref in enumerate(h_refs):

        @pl.when((i >= c * size) & (i < (c + 1) * size))
        def _(c=c, h_ref=h_ref):
            h_ref[pl.ds(i - c * size, value.shape[0])] = value


def fine_first(low, count, chunks, smoother, rhs):
    n, r, vb = rhs.shape
    size = count // chunks
    g = in_groups(size)
    steps = count // g

    def kernel(m_ref, rhs_ref, f_ref, *h_refs):
        def step(j, carry):
            at = j * g
            vs = [
                times(rhs_ref[low + at + i].astype(BF16), m_ref[low + at + i]) for i in range(g)
            ]
            for i in range(g):
                f_ref[at + i] = vs[i]
            store_chunks(at, jnp.stack([v.astype(BF16) for v in vs]), h_refs)
            return carry

        lax.fori_loop(0, steps, step, 0)

    f, *h = pl.pallas_call(
        kernel,
        in_specs=[VMEM] * 2,
        out_specs=[VMEM] * (1 + chunks),
        out_shape=[sds((count, r, vb), F32)] + [sds((size, r, vb), BF16)] * chunks,
        compiler_params=params(12),
        cost_estimate=cost(count * 0.04),
    )(smoother, rhs)
    return f, h


def brought(source, after):
    n = source.shape[0]
    parts = in_groups(n)
    size = n // parts

    def kernel(source_ref, after_ref, copied_ref, sems):
        copies = []
        for p in range(parts):
            at = pl.ds(p * size, size)
            copies.append(pltpu.make_async_copy(source_ref.at[at], copied_ref.at[at], sems.at[p]))
        for copy in copies:
            copy.start()
        for copy in copies:
            copy.wait()

    return pl.pallas_call(
        kernel,
        in_specs=[ANY] * 2,
        out_specs=VMEM,
        out_shape=sds(source.shape, source.dtype),
        scratch_shapes=[pltpu.SemaphoreType.DMA((parts,))],
        compiler_params=params(12),
        cost_estimate=cost(3),
    )(source, after)


def fine_sweep(low, count, chunks, cols, x_parts, tiles, smoother, rhs, field):
    n, r, vb = rhs.shape
    size = count // chunks
    g = in_groups(size)
    steps = count // g
    parts = len(x_parts)

    def kernel(cols_ref, *refs):
        x_refs, (t_ref, m_ref, rhs_ref, v_ref, f_ref), (*h_refs, x_ref) = (
            refs[:parts],
            refs[parts : parts + 5],
            refs[parts + 5 :],
        )
        fill_pair(x_ref, x_refs, n)
        ring = first_before(n, True)

        def step(j, carry):
            at = j * g
            zs = []
            for i in range(g):
                row = low + at + i
                z = rhs_ref[row] - row_product(cols_ref, row, ring, x_ref, t_ref)
                zs.append(z.astype(BF16))
            vs = [v_ref[at + i] + times(zs[i], m_ref[low + at + i]) for i in range(g)]
            for i in range(g):
                f_ref[at + i] = vs[i]
            store_chunks(at, jnp.stack([v.astype(BF16) for v in vs]), h_refs)
            return carry

        lax.fori_loop(0, steps, step, 0)

    f, *h = pl.pallas_call(
        kernel,
        in_specs=[SMEM] + [VMEM] * (parts + 4),
        out_specs=[VMEM] * (1 + chunks),
        out_shape=[sds((count, r, vb), F32)] + [sds((size, r, vb), BF16)] * chunks,
        scratch_shapes=[pltpu.VMEM((3 * n, r, vb), BF16)],
        compiler_params=params(12),
        cost_estimate=cost(count * 0.15),
    )(cols, *x_parts, tiles, smoother, rhs, field)
    return f, h


def one_hot(slots_row, vb):
    return (lax.broadcasted_iota(jnp.int32, (vb, vb), 0) == slots_row).astype(F32).astype(BF16)


def collected(z, slots_row):
    r, vb = z.shape
    high = z.astype(BF16)
    low = (z - high.astype(F32)).astype(BF16)
    both = times(jnp.concatenate([high, low], axis=0), one_hot(slots_row, vb))
    return both[:r] + both[r:]


def fine_restrict(cols, to_mid, x_parts, pack, rhs, slots, map_row, n1):
    n, r, vb = rhs.shape
    g = in_groups(n)
    steps = n // g
    parts = len(x_parts)
    blks = lax.axis_size("blk")
    pairs = blks // 2
    half = pairs * n1
    map_rows = -(-n // vb)
    cut = (pairs + 1) // 2

    def kernel(cols_ref, to_ref, *refs):
        x_refs, refs = refs[:parts], refs[parts:]
        pack_ref, rhs_ref, s_ref, map_ref, z_ref, own_ref, *others, table_ref, x_ref, acc_ref = refs
        fill_pair(x_ref, x_refs, n)
        acc_ref[...] = jnp.zeros_like(acc_ref)
        table_ref[:n] = s_ref[...]
        for q in range(map_rows):
            size = min(vb, n - q * vb)
            table_ref[n + q : n + q + 1, :size] = map_ref[:, q * vb : q * vb + size]
        ring = first_before(n, True)
        side = lax.axis_index("blk") % 2
        base = lax.axis_index("fold") * (blks * n1)

        def step(j, carry):
            at = j * g
            zs = [
                rhs_ref[at + i] - packed_product(cols_ref, at + i, ring, x_ref, pack_ref)
                for i in range(g)
            ]
            for i in range(g):
                z_ref[at + i] = zs[i]
            pieces = [collected(zs[i], s_ref[pl.ds(at + i, 1), :]) for i in range(g)]
            for i in range(g):
                to = to_ref[at + i] - base
                blk = to // n1
                apart = jnp.where(blk % 2 == side, 0, half)
                acc_ref[apart + (blk // 2) * n1 + (to - blk * n1)] += pieces[i]
            return carry

        lax.fori_loop(0, steps, step, 0)
        own_ref[...] = acc_ref[:half]
        pair = lax.axis_index("blk") // 2
        for q in range(pairs):
            at = pl.ds(half + (pair + pairs - 1 - q) % pairs * n1, n1)
            place = q % cut * n1
            others[q // cut][place : place + n1] = acc_ref[at].astype(BF16)

    return pl.pallas_call(
        kernel,
        in_specs=[SMEM] * 2 + [VMEM] * (parts + 4),
        out_specs=[VMEM] * 5,
        out_shape=[
            sds(rhs.shape, F32),
            sds((half, r, vb), F32),
            sds((cut * n1, r, vb), BF16),
            sds(((pairs - cut) * n1, r, vb), BF16),
            sds((n + map_rows, vb), jnp.int32),
        ],
        scratch_shapes=[pltpu.VMEM((3 * n, r, vb), BF16), pltpu.VMEM((2 * half, r, vb), F32)],
        compiler_params=params(16),
        cost_estimate=cost(n * 0.15),
    )(cols, to_mid, *x_parts, pack, rhs, slots, map_row)


def pair_sums(own, got, last, n1):
    half, r, vb = own.shape
    count = got.shape[0] // n1

    def kernel(own_ref, got_ref, *refs):
        pair = lax.axis_index("blk") // 2
        for k in range(count):
            at = pl.ds((pair + last - k) % (half // n1) * n1, n1)
            total = own_ref[at] + got_ref[k * n1 : (k + 1) * n1].astype(F32)
            refs[k][...] = total.astype(BF16)

    return pl.pallas_call(
        kernel,
        in_specs=[VMEM] * 2,
        out_specs=[VMEM] * count,
        out_shape=[sds((n1, r, vb), BF16)] * count,
        compiler_params=params(12),
        cost_estimate=cost(0.2),
    )(own, got)


def fine_last(cols, to_mid, slots, tables, mid_parts, pack, resid, fields, others):
    n, r, vb = resid.shape
    g = in_groups(fields[0].shape[0])
    steps = n // g
    wide = next(w for w in (16, 12, 8, 6, 4, 3, 2, 1) if n % w == 0)
    parts = len(mid_parts)
    half = parts // 2
    n1 = mid_parts[0].shape[0]

    def kernel(cols_ref, to_ref, near_to_ref, far_to_ref, s_ref, near_ref, far_ref, *refs):
        mid_refs, (pack_ref, z_ref), refs = refs[:parts], refs[parts : parts + 2], refs[parts + 2 :]
        v_refs, refs = refs[: len(fields)], refs[len(fields) :]
        other_refs, (out_hbm, *other_hbm), (f_ref, x_ref, all_ref, sems, other_sems) = (
            refs[: len(others)],
            refs[len(others) : 2 * len(others) + 1],
            refs[2 * len(others) + 1 :],
        )
        other_copies = [
            pltpu.make_async_copy(source, dest, other_sems.at[q])
            for q, (source, dest) in enumerate(zip(other_refs, other_hbm))
        ]
        for copy in other_copies:
            copy.start()

        def out_copy(j):
            at = pl.ds(j * g, g)
            return pltpu.make_async_copy(f_ref.at[at], out_hbm.at[at], sems.at[j])

        blk = lax.axis_index("blk")
        side = blk % 2
        base = lax.axis_index("fold") * (parts * n1)
        for p in range(parts):
            owner = (blk // 2 + half - p % half) % half * 2 + (side if p < half else 1 - side)
            all_ref[pl.ds(owner * n1, n1)] = mid_refs[parts - 1 - p][...].astype(F32)

        def lift(start, slots_of, to_of):
            def some(j, carry):
                lifted = []
                for q in range(wide):
                    index = jnp.broadcast_to(slots_of[pl.ds(j * wide + q, 1), :], (r, vb))
                    h = all_ref[to_of(j * wide + q) - base]
                    lifted.append(jnp.take_along_axis(h, index, axis=1))
                for q in range(wide):
                    x_ref[start + j * wide + q] = lifted[q].astype(BF16)
                return carry

            lax.fori_loop(0, n // wide, some, 0)

        def from_table(ref):
            if n <= vb:
                return lambda i: ref[n, i]
            return lambda i: ref[n + i // vb, i % vb]

        lift(n, s_ref, lambda i: to_ref[i])
        lift((1 - side) * (2 * n), near_ref, from_table(near_to_ref))
        lift(side * (2 * n), far_ref, from_table(far_to_ref))
        ring = first_before(n, True)

        def step(j, v_ref, low):
            at = j * g
            zs = [
                z_ref[at + i] - packed_product(cols_ref, at + i, ring, x_ref, pack_ref)
                for i in range(g)
            ]
            vs = [smoothed(zs[i], pack_ref, at + i) for i in range(g)]
            for i in range(g):
                f_ref[at + i] = vs[i] + (v_ref[at - low + i] + x_ref[n + at + i].astype(F32))
            out_copy(j).start()

        low = 0
        for v_ref in v_refs:
            high = low + v_ref.shape[0]

            def some_rows(j, carry, v_ref=v_ref, low=low):
                step(j, v_ref, low)
                return carry

            lax.fori_loop(low // g, high // g, some_rows, 0)
            low = high
        for j in range(steps):
            out_copy(j).wait()
        for copy in other_copies:
            copy.wait()

    return pl.pallas_call(
        kernel,
        in_specs=[SMEM] * 4 + [VMEM] * (5 + parts + len(fields) + len(others)),
        out_specs=[ANY] * (1 + len(others)),
        out_shape=[sds(resid.shape, F32)] + [sds(a.shape, a.dtype) for a in others],
        scratch_shapes=[
            pltpu.VMEM((n, r, vb), F32),
            pltpu.VMEM((3 * n, r, vb), BF16),
            pltpu.VMEM((parts * n1, r, vb), F32),
            pltpu.SemaphoreType.DMA((steps,)),
            pltpu.SemaphoreType.DMA((len(others),)),
        ],
        compiler_params=params(16),
        cost_estimate=cost(n * 0.2),
    )(
        cols,
        to_mid,
        *tables,
        slots,
        *tables,
        *mid_parts[::-1],
        pack,
        resid,
        *fields,
        *others,
    )


def packed(tiles, smoother, after):
    n, kt, vb, _ = tiles.shape

    def kernel(t_ref, m_ref, after_ref, o_ref):
        def one(i, carry):
            for k in range(kt):
                o_ref[i, k] = t_ref[i, k].T
            o_ref[i, kt] = m_ref[i].T
            return carry

        lax.fori_loop(0, n, one, 0)

    return pl.pallas_call(
        kernel,
        in_specs=[VMEM] * 2 + [ANY],
        out_specs=VMEM,
        out_shape=sds((n, kt + 1, vb, vb), BF16),
        compiler_params=params(12),
        cost_estimate=cost(2),
    )(tiles, smoother, after)


def add_and_smooth(pack, terms):
    shape = terms[0].shape

    def kernel(pack_ref, *refs):
        term_refs, (rhs_ref, f_ref, h_ref) = refs[:-3], refs[-3:]
        totals = []
        for i in range(shape[0]):
            total = term_refs[0][i].astype(F32)
            for t in term_refs[1:]:
                total = total + t[i].astype(F32)
            totals.append(total)
        vs = [smoothed(total, pack_ref, i) for i, total in enumerate(totals)]
        for i, v in enumerate(vs):
            rhs_ref[i] = totals[i]
            f_ref[i] = v
            h_ref[i] = v.astype(BF16)

    return pl.pallas_call(
        kernel,
        in_specs=[VMEM] * (1 + len(terms)),
        out_specs=[VMEM] * 3,
        out_shape=[sds(shape, F32), sds(shape, F32), sds(shape, BF16)],
        compiler_params=params(12),
        cost_estimate=cost(0.3),
    )(pack, *terms)


def less_own(pack, rhs, x):
    def kernel(pack_ref, rhs_ref, x_ref, z_ref):
        own = x_ref[...].astype(F32)
        for i in range(rhs.shape[0]):
            z_ref[i] = rhs_ref[i] - lax.dot_general(
                own[i].astype(BF16), pack_ref[i, 0], NN, preferred_element_type=F32
            )

    return pl.pallas_call(
        kernel,
        in_specs=[VMEM] * 3,
        out_specs=VMEM,
        out_shape=sds(rhs.shape, F32),
        compiler_params=params(12),
        cost_estimate=cost(0.3),
    )(pack, rhs, x)


def small_sweep(folded, cols, x3, pack, rhs, field, last=False):
    n, r, vb = rhs.shape
    pick = BF16 if r % 16 == 0 else F32
    kinds = [BF16] if last else [BF16, F32]
    skip = 1 if folded in SPLIT else 0
    if skip:
        rhs = less_own(pack, rhs, x3[1])

    def kernel(cols_ref, c_ref, b_ref, a_ref, pack_ref, rhs_ref, v_ref, *refs):
        out_refs, x_ref = refs[:-1], refs[-1]
        fill(x_ref, (a_ref, b_ref, c_ref))
        ring = first_before(n, folded)
        zs = [rhs_ref[i] - packed_product(cols_ref, i, ring, x_ref, pack_ref, skip) for i in range(n)]
        vs = [v_ref[i] + smoothed(zs[i], pack_ref, i) for i in range(n)]
        for i, v in enumerate(vs):
            for out_ref in out_refs:
                out_ref[i] = v.astype(out_ref.dtype)

    return pl.pallas_call(
        kernel,
        in_specs=[SMEM] + [VMEM] * 6,
        out_specs=[VMEM] * len(kinds),
        out_shape=[sds(rhs.shape, kind) for kind in kinds],
        scratch_shapes=[pltpu.VMEM((3 * n, r, vb), pick)],
        compiler_params=params(12),
        cost_estimate=cost(1),
    )(cols, *x3[::-1], pack, rhs, field)


def mid_restrict(cols, to_low, x3, pack, rhs, slots, lows):
    n, r, vb = rhs.shape
    folds = lax.axis_size("fold")
    share = r // folds

    def kernel(cols_ref, to_ref, c_ref, b_ref, a_ref, pack_ref, rhs_ref, s_ref, *refs):
        outs, (x_ref, acc_ref, cut_ref) = refs[:folds], refs[folds:]
        fill(x_ref, (a_ref, b_ref, c_ref))
        acc_ref[...] = jnp.zeros_like(acc_ref)
        ring = first_before(n, True)
        zs = [rhs_ref[i] - packed_product(cols_ref, i, ring, x_ref, pack_ref) for i in range(n)]
        pieces = [collected(zs[i], s_ref[i : i + 1, :]) for i in range(n)]
        base = lax.axis_index("blk") * lows
        for i in range(n):
            acc_ref[to_ref[i] - base] += pieces[i]
        for f in range(folds):
            cut_ref[f] = acc_ref[:, f * share : (f + 1) * share, :]
        for f in range(folds):
            outs[f][...] = cut_ref[(lax.axis_index("fold") + f) % folds].astype(BF16)

    return pl.pallas_call(
        kernel,
        in_specs=[SMEM] * 2 + [VMEM] * 6,
        out_specs=[VMEM] * folds,
        out_shape=[sds((lows, share, vb), BF16)] * folds,
        scratch_shapes=[
            pltpu.VMEM((3 * n, r, vb), BF16),
            pltpu.VMEM((lows, r, vb), F32),
            pltpu.VMEM((folds, lows, share, vb), F32),
        ],
        compiler_params=params(12),
    )(cols, to_low, *x3[::-1], pack, rhs, slots)


def mid_lift(to_low, parts, field, slots):
    n, r, vb = field.shape
    folds = len(parts)
    lows, share = parts[0].shape[:2]

    def kernel(to_ref, *refs):
        part_refs, (v_ref, s_ref, c_ref, f_ref, h_ref, cut_ref) = refs[:folds], refs[folds:]
        for f in range(folds):
            owner = (lax.axis_index("fold") + folds - f) % folds
            cut_ref[owner] = part_refs[f][...].astype(F32)
        for f in range(folds):
            c_ref[:, f * share : (f + 1) * share, :] = cut_ref[f]
        for i in range(n):
            index = jnp.broadcast_to(s_ref[i : i + 1, :], (r, vb))
            low = to_ref[i] - lax.axis_index("blk") * lows
            v = v_ref[i] + jnp.take_along_axis(c_ref[low], index, axis=1)
            f_ref[i] = v
            h_ref[i] = v.astype(BF16)

    return pl.pallas_call(
        kernel,
        in_specs=[SMEM] + [VMEM] * (folds + 2),
        out_specs=[VMEM] * 3,
        out_shape=[sds((lows, r, vb), F32), sds(field.shape, F32), sds(field.shape, BF16)],
        scratch_shapes=[pltpu.VMEM((folds, lows, share, vb), F32)],
        compiler_params=params(16),
    )(to_low, *parts, field, slots)


def on_device(
    fine_rhs,
    fine_tiles,
    fine_cols,
    fine_smoother,
    fine_map,
    fine_slots,
    mid_tiles,
    mid_cols,
    mid_smoother,
    mid_map,
    mid_slots,
    coarse_tiles,
    coarse_cols,
    coarse_smoother,
):
    n0, r, vb = fine_rhs.shape
    n1 = mid_tiles.shape[0]
    n2 = coarse_tiles.shape[0]
    blks, folds = lax.axis_size("blk"), lax.axis_size("fold")
    pairs = blks // 2
    cols0, cols1, cols2 = fine_cols.T, mid_cols.T, coarse_cols.T

    halves, chunks = HALVES, CHUNKS
    count = n0 // halves
    v, h = [], []
    for k in range(halves):
        part, rough = fine_first(k * count, count, chunks, fine_smoother, fine_rhs)
        v.append(part)
        h += rough
    x = h + pair_halos(h)
    fine_tiles = brought(fine_tiles, x[2 * halves * chunks])
    down, h = [], []
    for k in range(halves):
        part, rough = fine_sweep(
            k * count, count, chunks, cols0, x, fine_tiles, fine_smoother, fine_rhs, v[k]
        )
        down.append(part)
        h += rough
    x = h + pair_halos(h)
    fine_pack = packed(fine_tiles, fine_smoother, x[2 * halves * chunks - 1])
    resid, own, *others, table = fine_restrict(
        cols0, fine_map, x, fine_pack, fine_rhs, fine_slots, fine_map[None], n1
    )
    steps = [[(i, (i + 2 * k) % blks) for i in range(blks)] for k in range(pairs)]
    late = partner(others[1])
    early = partner(others[0])
    early, near = lax.optimization_barrier((early, partner(table)))
    mid_pack = packed(mid_tiles, mid_smoother, others[0])
    low_pack = packed(coarse_tiles, coarse_smoother, others[0])
    early, mid_pack, low_pack = lax.optimization_barrier((early, mid_pack, low_pack))
    cut = others[1].shape[0] // n1
    sums = pair_sums(own, early, pairs - 1, n1) + pair_sums(own, late, cut - 1, n1)
    sums = sums[::-1]
    terms = [sums[0]] + [lax.ppermute(sums[k], "blk", steps[k]) for k in range(1, pairs)]

    mid_rhs, w, h = add_and_smooth(mid_pack, terms)
    before, after = halos(h)
    w, h = small_sweep(True, cols1, (before, h, after), mid_pack, mid_rhs, w)[::-1]
    before, after = halos(h)
    cuts = mid_restrict(cols1, mid_map, (before, h, after), mid_pack, mid_rhs, mid_slots, n2)

    shifts = [[(i, (i + k) % folds) for i in range(folds)] for k in range(folds)]
    terms = [cuts[0]] + [lax.ppermute(cuts[k], "fold", shifts[k]) for k in range(1, folds)]
    terms, far = lax.optimization_barrier((terms, forwarded(near)))
    tables = [near, far]
    low_rhs, c, h = add_and_smooth(low_pack, terms)
    for k in range(1, COARSE):
        before, after = halos(h)
        h, *c = small_sweep(
            False, cols2, (before, h, after), low_pack, low_rhs, c, last=k == COARSE - 1
        )
        c = c[0] if c else None
    parts = [h] + [lax.ppermute(h, "fold", shifts[k]) for k in range(1, folds)]

    coarse_field, w, h = mid_lift(mid_map, parts, w, mid_slots)
    before, after = halos(h)
    h, mid_field = small_sweep(True, cols1, (before, h, after), mid_pack, mid_rhs, w)

    far_mids = [lax.ppermute(h, "blk", steps[k]) for k in range(pairs - 1, 0, -1)]
    mids = [h] + far_mids[::-1]
    mids = mids + [partner(m) for m in far_mids + [h]][::-1]
    fine_field, mid_field, coarse_field = fine_last(
        cols0,
        fine_map,
        fine_slots,
        tables,
        mids,
        fine_pack,
        resid,
        down,
        (mid_field, coarse_field),
    )
    return fine_field, mid_field, coarse_field


def solution(mesh):
    both = ("fold", "blk")
    return jax.shard_map(
        on_device,
        mesh=mesh,
        in_specs=(
            P(both, None, None),
            P(both, None, None, None),
            P(both, None),
            P(both, None, None),
            P(both),
            P(both, None),
            P(both, None, None, None),
            P(both, None),
            P(both, None, None),
            P(both),
            P(both, None),
            P("blk", None, None, None),
            P("blk", None),
            P("blk", None, None),
        ),
        out_specs=(P(both, None, None), P(both, None, None), P("blk", None, None)),
        check_vma=False,
    )
```
